128 devices in a mesh: north: 4 (over z), east: 32 (over x, y, core).
Axes of the slice: x: 4, y: 4, z: 4, core: 2. Of those that a mesh axis runs over, the one named last changes fastest.
Arguments:
- destinations: int32 [32768, 1], P(('north', 'east')), may hold values from 0 to 127; in each aligned block of 256 rows (0 to 255, 256 to 511, ...) at most 4 rows name the same one
- cells: int32 [32768, 128], P(('north', 'east')), may hold values from 0 to 16128
- fractions: float32 [32768, 2, 128], P(('north', 'east')), may hold values from 0 to 1
- weights: float32 [32768, 128], P(('north', 'east')), may hold values from 0.1 to 10
- heights: float32 [32768, 128], P(('north', 'east')), may hold values from -6 to 6
- counts: int32 [128], P(('north', 'east')), may hold values from 1 to 256, 28672 in all
Outputs:
- surface: float32 [512, 4096], P('north', 'east')
- residual: float32 [512, 4096], P('north', 'east')
The draws below stay inside these ranges and needn't reach their ends.
Inputs may be any that keep to these rules, and one draw needn't show every extreme that they name: `destinations`: among the 256 blocks of one holder no tile is named by more than 4 blocks, and 4 is reached; every tile is named by some block. `cells`: k names cell row k // 127 and column k % (127) of the block's tile, so all four corner nodes of a return lie in that tile. Holder h holds live blocks 0 to counts[h] - 1; the largest count is 256.
All inputs are finite; a program needn't handle non-finite values.
Results may differ from the reference program's by a relative error of at most 0.00028.
Values sent between devices are 32-bit elements; how exact they have to be, the bound alone decides.
No kernel may reach another device: no remote copies, remote signals or barrier semaphores. Data moves between devices by JAX's collectives and lax.ppermute only.
A program may use at most 64 MiB of HBM per device.

```python
import math
import jax
import jax.numpy as jnp
import numpy as np

TR = 128
TC = 128
BLK_DEV = 256
RETURNS = 128
MOST = 4
ITERS = 3
NR = 512
NC = 4096
BLOCKS = 32768
N_NORTH = 4
N_EAST = 32


def place_ends(drawn, key, low, high):
    longest = drawn.shape.index(max(drawn.shape))
    spots = []
    for shift in (0, 1):
        where = [jax.random.randint(jax.random.fold_in(key, axis), (), 0, length) for axis, length in enumerate(drawn.shape)]
        where[longest] = (where[longest] + shift) % drawn.shape[longest]
        spots.append(tuple(where))
    return drawn.at[spots[0]].set(low).at[spots[1]].set(high)


def block_scale(key, dims, cuts, least, largest):
    level, own = 1.0, jax.random.fold_in(key, 6)
    for position, shards_of in cuts:
        steps = jnp.exp(jax.random.uniform(jax.random.fold_in(own, position), (shards_of,), jnp.float32, least / len(cuts), largest / len(cuts)))
        level = level * jnp.repeat(steps, dims[position] // shards_of).reshape([-1 if axis == position else 1 for axis in range(len(dims))])
    return level


def length_profile(count, total, limit, lean):
    portions = [(1 << 20) // math.isqrt(grade ** lean) + 1 for grade in range(2, count + 1)]
    rest, given = total - limit - (count - 1), [1] * (count - 1)
    while rest > 0:
        candidates = [i for i in range(count - 1) if given[i] < limit]
        pool, remaining = sum([portions[i] for i in candidates]), rest
        for i in candidates:
            extra = min(limit - given[i], max(1, remaining * portions[i] // pool), rest)
            given[i] = given[i] + extra
            rest = rest - extra
    return np.array([limit] + given)


def uneven(own_key, number_of, total, reach, lean):
    if number_of == 2:
        one = jax.random.randint(own_key, (), max(1, total - reach), min(reach, total - 1) + 1)
        return jnp.stack([one, total - one])
    lengths = jnp.asarray(length_profile(number_of, total, reach, lean), jnp.int32)
    twos = (number_of - 1) // 2
    source_of, taker = lengths[1:1 + 2 * twos:2], lengths[2:2 + 2 * twos:2]
    slack = jnp.minimum(source_of - 1, reach - taker)
    shifted = jax.random.randint(jax.random.fold_in(own_key, 1), (twos,), 0, 1 << 20) % (slack + 1)
    lengths = lengths.at[1:1 + 2 * twos:2].set(source_of - shifted).at[2:2 + 2 * twos:2].set(taker + shifted)
    return lengths[jax.random.permutation(jax.random.fold_in(own_key, 2), number_of)]


def routed_block(stream_key, own, number, rows, number_of, top, bound, lean):
    order = jax.random.permutation(stream_key, number_of)
    packed, common = portions_of(number_of, rows * top, bound, lean, True), portions_of(number_of, rows * top, bound, lean, False)
    places = jnp.arange(number_of)

    def named(lengths, rotation):
        used = int((lengths > 0).sum())
        fixed = max(1, used // 4)
        moved = fixed + (places - fixed + rotation * (used - fixed)) % max(1, number_of - fixed)
        return jnp.zeros((number_of,), jnp.int32).at[order[jnp.where(places < fixed, places, moved)]].set(jnp.asarray(lengths, jnp.int32))

    lengths = jnp.where(number % 4 == 0, named(packed, number // 4), named(common, number - number // 4 - 1))
    mixed = jax.random.permutation(jax.random.fold_in(own, 3), number_of)
    giver, taker = mixed[0:number_of // 2 * 2:2], mixed[1:number_of // 2 * 2:2]
    slack = jnp.minimum(lengths[giver] - 1, bound - lengths[taker]) // 2
    slack = jnp.where((giver == order[0]) | (taker == order[0]) | (lengths[taker] == 0), 0, jnp.maximum(slack, 0))
    moved = jax.random.randint(jax.random.fold_in(own, 4), (number_of // 2,), 0, 1 << 20) % (slack + 1)
    lengths = lengths.at[giver].add(-moved).at[taker].add(moved)
    members = jnp.searchsorted(jnp.cumsum(lengths), jnp.arange(rows * top), side="right").astype(jnp.int32)
    table = members.reshape(top, rows).T
    table = table[jax.random.permutation(jax.random.fold_in(own, 1), rows)]
    rotation = jax.random.randint(jax.random.fold_in(own, 2), (rows, 1), 0, top)
    return jnp.take_along_axis(table, (jnp.arange(top)[None, :] + rotation) % top, axis=1)


def portions_of(count, total, reach, slope, full):
    portions = [(1 << 20) // math.isqrt(standing ** slope) + 1 for standing in range(1, count + 1)]
    largest = reach if full else min(reach, max(-(-total // count), total * portions[0] // sum(portions)))
    least = 1 if total - largest >= count - 1 else 0
    given, surplus = [largest] + [least] * (count - 1), total - largest - least * (count - 1)
    while surplus > 0:
        movable = [i for i in range(1, count) if given[i] < largest] or [i for i in range(1, count) if given[i] < reach]
        pool, left = sum([portions[i] for i in movable]), surplus
        for i in movable:
            addition = min(reach - given[i], max(1, left * portions[i] // pool), surplus)
            given[i] = given[i] + addition
            surplus = surplus - addition
    return np.array(given)


def bell_draw(key, dims, scale, most, pieces=(), kind=jnp.bfloat16):
    factor_of = block_scale(key, dims, pieces, -0.22, 0.18) if pieces else 1.0
    values = jax.random.normal(key, dims, jnp.float32) * scale * factor_of
    return jnp.minimum(jnp.maximum(values, -most), most).astype(kind)


def setup_inputs(seed: int = 0) -> dict:
    keys = jax.random.split(jax.random.key(seed), 7)
    destinations_keys = jax.random.split(jax.random.fold_in(keys[0], 1), BLOCKS // BLK_DEV)
    destinations_turns = jax.random.permutation(jax.random.fold_in(keys[0], 3), BLOCKS // BLK_DEV)
    destinations = jax.vmap(lambda own, number: routed_block(jax.random.fold_in(keys[0], 2), own, number, BLK_DEV, N_NORTH * N_EAST, 1, MOST, 2))(destinations_keys, destinations_turns).reshape((BLOCKS, 1))
    cells = place_ends(jax.random.randint(keys[1], (BLOCKS, RETURNS), 0, (TR - 1) * (TC - 1)), jax.random.fold_in(keys[1], 1), 0, ((TR - 1) * (TC - 1)) - 1).astype(jnp.int32)
    fractions = jnp.clip(1.0 * jax.random.uniform(keys[2], (BLOCKS, 2, RETURNS), jnp.float32) ** block_scale(keys[2], (BLOCKS, 2, RETURNS), ((0, 128),), -0.2, 0.2), 0.0, 1.0)
    weights = jnp.clip(jnp.exp(math.log(10.0) - 4.6051702 * jax.random.uniform(keys[3], (BLOCKS, RETURNS), jnp.float32) ** block_scale(keys[3], (BLOCKS, RETURNS), ((0, 128),), -0.2, 0.2)), 0.1, 10.0)
    heights = bell_draw(keys[4], (BLOCKS, RETURNS), 1.0, 6.0, ((0, 128),), jnp.float32)
    counts = uneven(keys[5], N_NORTH * N_EAST, N_NORTH * N_EAST * BLK_DEV * 7 // 8, BLK_DEV, 1).astype(jnp.int32)
    return dict(destinations=destinations, cells=cells, fractions=fractions, weights=weights, heights=heights, counts=counts)


smooth_weight = 1.0
tension = 0.75


def laplace(field):
    padded = jnp.pad(field, 1)
    return padded[2:, 1:-1] + padded[:-2, 1:-1] + padded[1:-1, 2:] + padded[1:-1, :-2] - 4.0 * field


def regular(field):
    inner = laplace(field)
    return smooth_weight * ((1.0 - tension) * laplace(inner) - tension * inner)


def reference(destinations, cells, fractions, weights, heights, counts):
    blocks = destinations.shape[0]
    holder = jnp.arange(blocks, dtype=jnp.int32) // BLK_DEV
    within = jnp.arange(blocks, dtype=jnp.int32) % BLK_DEV
    live = (within < counts[holder]).astype(jnp.float32)
    tile = destinations[:, 0]
    rows = (tile // N_EAST)[:, None] * TR + cells // (TC - 1)
    cols = (tile % N_EAST)[:, None] * TC + cells % (TC - 1)
    base = (rows * NC + cols).reshape(-1).astype(jnp.int32)
    down = fractions[:, 0, :].reshape(-1)
    right_off = fractions[:, 1, :].reshape(-1)
    index = jnp.stack([base, base + NC, base + 1, base + NC + 1])
    share = jnp.stack([(1.0 - down) * (1.0 - right_off), down * (1.0 - right_off), (1.0 - down) * right_off, down * right_off])
    mass = (weights * live[:, None]).reshape(-1)
    height = heights.reshape(-1)

    def interp(field):
        return jnp.sum(share * field.reshape(-1)[index], axis=0)

    def spread(values):
        total = jnp.zeros((NR * NC,), jnp.float32)
        total = total.at[index.reshape(-1)].add((share * values[None, :]).reshape(-1))
        return total.reshape(NR, NC)

    def operate(field):
        return spread(mass * interp(field)) + regular(field)

    right = spread(mass * height)
    surface = jnp.zeros((NR, NC), jnp.float32)
    residual = right
    direction = right
    norm_now = jnp.sum(residual * residual)
    for step in range(ITERS):
        image = operate(direction)
        alpha = norm_now / jnp.sum(direction * image)
        surface = surface + alpha * direction
        residual = residual - alpha * image
        norm_next = jnp.sum(residual * residual)
        direction = residual + (norm_next / norm_now) * direction
        norm_now = norm_next
    return surface, residual
```

```python
import jax
import jax.numpy as jnp
from jax import lax
from jax.experimental import pallas as pl
from jax.experimental.pallas import tpu as pltpu
from jax.sharding import PartitionSpec as P

TR = 128
TC = 128
BLK_DEV = 256
MOST = 4
N_NORTH = 4
N_EAST = 32
TILES = N_NORTH * N_EAST
SHRINK = 1.0 / 64.0
TENSION = 0.75
AXES = ("north", "east")
f32 = jnp.float32
bf16 = jnp.bfloat16

SLOTS = 8
CHUNKS = TILES * MOST // SLOTS
SPAN = SLOTS * 128
BANDS = 16
LEFT_ROWS = BANDS * 64 + 16


def whole(space=pltpu.VMEM):
    return pl.BlockSpec(memory_space=space)


def route_kernel(dest_ref, count_ref, cells_ref, frac_ref, weight_ref, height_ref, out_ref, seen_ref):
    out_ref[...] = jnp.zeros_like(out_ref)

    def clear(k, _):
        seen_ref[k] = 0
        return 0

    lax.fori_loop(0, TILES, clear, 0, unroll=8)

    def place(b, _):
        tile = dest_ref[b]
        rank = seen_ref[tile]
        seen_ref[tile] = rank + 1
        row = pl.ds(b, 1)
        to = pl.ds(rank, 1)
        out_ref[tile, 0, to, :] = cells_ref[row, :].astype(f32)
        out_ref[tile, 1, to, :] = frac_ref[b, 0:1, :]
        out_ref[tile, 2, to, :] = frac_ref[b, 1:2, :]
        out_ref[tile, 3, to, :] = weight_ref[row, :]
        out_ref[tile, 4, to, :] = height_ref[row, :]
        return 0

    lax.fori_loop(0, count_ref[0], place, 0)


def high_low(value):
    high = value.astype(bf16).astype(f32)
    return [high, value - high]


def build(chunk, x_ref, vals_ref, left_ref, right_ref):
    def field(f):
        return jnp.concatenate([x_ref[2 * chunk, f], x_ref[2 * chunk + 1, f]], axis=0)

    cell, d, e, mass, height = [field(f) for f in range(5)]
    i = jnp.floor((cell + 0.5) * (1.0 / 127.0))
    j = cell - 127.0 * i
    lower = i >= 64.0
    i_in = jnp.where(lower, i - 64.0, i)
    place = j + jnp.where(lower, 128.0, 0.0)
    a0, a1, b0, b1 = 1.0 - d, d, 1.0 - e, e
    mh = mass * height
    cols = [mass * b0 * b0, mass * b1 * b1, mass * b0 * b1]
    ends = [mh * b0, mh * b1]
    down, up, mid = [], [], []
    for c in cols:
        down += high_low(c * a1 * a1)
        up += high_low(c * a0 * a0)
        mid += high_low(c * a0 * a1)
    for c in ends:
        down += high_low(c * a1)
        up += high_low(c * a0)
    stack = down + up + mid + [i_in, place]
    for k, v in enumerate(stack):
        vals_ref[k * SLOTS:(k + 1) * SLOTS, :] = v
    iota = lax.broadcasted_iota(jnp.int32, (16, 128), 0).astype(f32).astype(bf16)
    zero = jnp.zeros((16, 128), bf16)
    one = jnp.ones((16, 128), bf16)

    def row(k, s):
        return jnp.broadcast_to(vals_ref[k * SLOTS + s:k * SLOTS + s + 1, :], (16, 128))

    n = len(down)
    for s in range(SLOTS):
        lanes = slice(s * 128, (s + 1) * 128)
        i_row = row(26, s)
        i_b = i_row.astype(bf16)
        i_next = (i_row + 1.0).astype(bf16)
        at = [(iota + float(16 * g)) == i_b for g in range(4)]
        after = [(iota + float(16 * g)) == i_next for g in range(4)]
        for k in range(n):
            v1 = row(k, s).astype(bf16)
            v0 = row(n + k, s).astype(bf16)
            for g in range(4):
                left_ref[k * 64 + 16 * g:k * 64 + 16 * g + 16, lanes] = jnp.where(
                    at[g], v0, jnp.where(after[g], v1, zero))
        for k in range(6):
            v = row(2 * n + k, s).astype(bf16)
            base = (n + k) * 64
            for g in range(4):
                left_ref[base + 16 * g:base + 16 * g + 16, lanes] = jnp.where(at[g], v, zero)
        spill = vals_ref[pl.ds(s, 16, stride=SLOTS), :]
        left_ref[1024:1040, lanes] = jnp.where(i_row == 63.0, spill, 0.0).astype(bf16)
        p_b = row(27, s).astype(bf16)
        for g in range(16):
            right_ref[16 * g:16 * g + 16, lanes] = jnp.where((iota + float(16 * g)) == p_b, one, zero)


def shifted(a, by, axis):
    return pltpu.roll(a, by % a.shape[axis], axis)


def gather_kernel(x_ref, fields_ref, top_ref, bottom_ref, west_ref, east_ref,
                  vals_ref, left_ref, right_ref, acc_ref):
    acc_ref[...] = jnp.zeros_like(acc_ref)

    def multiply():
        acc_ref[...] += lax.dot_general(
            left_ref[...], right_ref[...], (((1,), (1,)), ((), ())),
            preferred_element_type=f32)

    def step(c, _):
        build(c, x_ref, vals_ref, left_ref, right_ref)
        multiply()
        return 0

    lax.fori_loop(0, CHUNKS, step, 0)

    row_ids = lax.broadcasted_iota(jnp.int32, (TR, TC), 0)

    def band(k):
        part = acc_ref[k * 64:(k + 1) * 64, :]
        full = jnp.concatenate([part[:, :128], part[:, 128:]], axis=0)
        if k < 10:
            extra = jnp.broadcast_to(acc_ref[1024 + k:1025 + k, 0:128], (TR, TC))
            full = full + jnp.where(row_ids == 64, extra, 0.0)
        return full

    def pair(k):
        return band(k) + band(k + 1)

    diag = pair(0) + shifted(pair(2), 1, 1)
    along_east = pair(4)
    rhs = pair(6) + shifted(pair(8), 1, 1)
    along_south = pair(10) + shifted(pair(12), 1, 1)
    cross = pair(14)
    for k, v in enumerate([rhs, diag, along_east, along_south, cross]):
        fields_ref[k] = v
        top_ref[k] = v[0:8]
        bottom_ref[k] = v[120:128]
        t = v.T
        west_ref[k] = t[0:8]
        east_ref[k] = t[120:128]


def corner_kernel(top_ref, bottom_ref, from_west_ref, from_east_ref, north_ref, south_ref):
    lane = lax.broadcasted_iota(jnp.int32, (8, 128), 1)
    for k in range(5):
        w = from_west_ref[k]
        e = shifted(from_east_ref[k], 64, 1)
        north_ref[k] = top_ref[k]
        south_ref[k] = bottom_ref[k]
        north_ref[5 + k] = jnp.where(lane < 64, w, e)
        south_ref[5 + k] = jnp.where(lane >= 64, w, e)


EXT_R = 144
EXT_C = 256


def krylov_kernel(place_ref, fields_ref, from_west_ref, from_east_ref, from_north_ref, from_south_ref,
                  basis_ref, moments_ref):
    gn = place_ref[0]
    ge = place_ref[1]
    rows = lax.broadcasted_iota(jnp.int32, (EXT_R, EXT_C), 0)
    cols = lax.broadcasted_iota(jnp.int32, (EXT_R, EXT_C), 1)
    grow = gn * TR + jnp.where(rows < 136, rows, rows - EXT_R)
    gcol = ge * TC + jnp.where(cols < 192, cols, cols - EXT_C)
    inside = (grow >= 0) & (grow < N_NORTH * TR) & (gcol >= 0) & (gcol < N_EAST * TC)

    ext = []
    for k in range(5):
        w = from_west_ref[k]
        e = from_east_ref[k]
        n = from_north_ref[5 + k]
        s = from_south_ref[5 + k]
        zeros = jnp.zeros((112, 128), f32)
        side = jnp.concatenate([e, zeros, w], axis=0).T
        n_e = shifted(n, 64, 1)
        s_e = shifted(s, 64, 1)
        south_side = jnp.concatenate([s_e, zeros, s], axis=0).T
        north_side = jnp.concatenate([n_e, zeros, n], axis=0).T
        left = jnp.concatenate([fields_ref[k], from_south_ref[k], from_north_ref[k]], axis=0)
        right = jnp.concatenate([side, south_side[0:8], north_side[120:128]], axis=0)
        full = jnp.concatenate([left, right], axis=1)
        ext.append(jnp.where(inside, full, 0.0))
    v0, diag, along_east, along_south, cross = ext

    def laplace(u, u_l, u_r, u_u, u_d):
        return jnp.where(inside, u_l + u_r + u_u + u_d - 4.0 * u, 0.0)

    def operate(u):
        u_r = shifted(u, -1, 1)
        u_l = shifted(u, 1, 1)
        u_d = shifted(u, -1, 0)
        u_u = shifted(u, 1, 0)
        lu = laplace(u, u_l, u_r, u_u, u_d)
        llu = laplace(lu, shifted(lu, 1, 1), shifted(lu, -1, 1), shifted(lu, 1, 0), shifted(lu, -1, 0))
        u_rd = shifted(u_r, -1, 0)
        out = diag * u + along_east * u_r + along_south * u_d + cross * u_rd
        out = out + shifted(along_east * u + cross * u_d, 1, 1)
        out = out + shifted(along_south * u + cross * u_r + shifted(cross * u, 1, 1), 1, 0)
        return (out + (1.0 - TENSION) * llu - TENSION * lu) * SHRINK

    v = [v0]
    for _ in range(3):
        v.append(operate(v[-1]))
    own = [a[0:TR, 0:TC] for a in v]
    for k in range(4):
        basis_ref[k] = own[k]
    pairs = [(0, 0), (0, 1), (1, 1), (1, 2), (2, 2), (2, 3)]
    lane = lax.broadcasted_iota(jnp.int32, (TILES, 128), 1)
    out = jnp.zeros((TILES, 128), f32)
    for k, (p, q) in enumerate(pairs):
        m = jnp.sum(jnp.sum(own[p] * own[q], axis=0, keepdims=True), axis=1, keepdims=True)
        out = jnp.where(lane == k, m, out)
    moments_ref[...] = out


def finish_kernel(moments_ref, basis_ref, surface_ref, residual_ref):
    total = jnp.sum(moments_ref[...], axis=0, keepdims=True)
    m = [total[:, k:k + 1] for k in range(6)]

    def dot(p, q, shift):
        terms = [p[a] * q[b] * m[a + b + shift] for a in range(len(p)) for b in range(len(q))]
        s = terms[0]
        for t in terms[1:]:
            s = s + t
        return s

    one = jnp.ones_like(m[0])
    res = [one]
    direction = [one]
    surf = []
    rr = m[0]
    for it in range(3):
        alpha = rr / dot(direction, direction, 1)
        surf = [(surf[k] if k < len(surf) else 0.0) + alpha * direction[k] for k in range(len(direction))]
        stepped = [jnp.zeros_like(one)] + [alpha * c for c in direction]
        res = [(res[k] if k < len(res) else 0.0) - stepped[k] for k in range(len(stepped))]
        if it < 2:
            fresh = dot(res, res, 0)
            beta = fresh / rr
            direction = [res[k] + (beta * direction[k] if k < len(direction) else 0.0) for k in range(len(res))]
            rr = fresh
    basis = [basis_ref[k] for k in range(4)]
    out = (surf[0] * SHRINK) * basis[0]
    for k in range(1, 3):
        out = out + (surf[k] * SHRINK) * basis[k]
    surface_ref[...] = out
    out = res[0] * basis[0]
    for k in range(1, 4):
        out = out + res[k] * basis[k]
    residual_ref[...] = out


def body(destinations, cells, fractions, weights, heights, counts):
    params = pltpu.CompilerParams(vmem_limit_bytes=40 * 1024 * 1024)
    send = pl.pallas_call(
        route_kernel,
        out_shape=jax.ShapeDtypeStruct((TILES, 5, MOST, 128), f32),
        in_specs=[whole(pltpu.SMEM), whole(pltpu.SMEM)] + [whole()] * 4,
        out_specs=whole(),
        scratch_shapes=[pltpu.SMEM((TILES,), jnp.int32)],
        compiler_params=params,
    )(destinations.reshape(BLK_DEV), counts, cells, fractions, weights, heights)
    got = lax.all_to_all(send, AXES, split_axis=0, concat_axis=0, tiled=True)
    strip = jax.ShapeDtypeStruct((5, 8, 128), f32)
    fields, top, bottom, west, east = pl.pallas_call(
        gather_kernel,
        out_shape=[jax.ShapeDtypeStruct((5, TR, TC), f32)] + [strip] * 4,
        in_specs=[whole()],
        out_specs=[whole()] * 5,
        scratch_shapes=[
            pltpu.VMEM((28 * SLOTS, 128), f32),
            pltpu.VMEM((LEFT_ROWS, SPAN), bf16),
            pltpu.VMEM((256, SPAN), bf16),
            pltpu.VMEM((LEFT_ROWS, 256), f32),
        ],
        compiler_params=params,
    )(got)
    up_e = [(i, (i + 1) % N_EAST) for i in range(N_EAST)]
    down_e = [(j, i) for i, j in up_e]
    up_n = [(i, (i + 1) % N_NORTH) for i in range(N_NORTH)]
    down_n = [(j, i) for i, j in up_n]
    from_west = lax.ppermute(east, "east", up_e)
    from_east = lax.ppermute(west, "east", down_e)
    message = jax.ShapeDtypeStruct((10, 8, 128), f32)
    to_north, to_south = pl.pallas_call(
        corner_kernel,
        out_shape=[message] * 2,
        in_specs=[whole()] * 4,
        out_specs=[whole()] * 2,
    )(top, bottom, from_west, from_east)
    from_north = lax.ppermute(to_south, "north", up_n)
    from_south = lax.ppermute(to_north, "north", down_n)
    place = jnp.stack([lax.axis_index("north"), lax.axis_index("east")]).astype(jnp.int32)
    basis, moments = pl.pallas_call(
        krylov_kernel,
        out_shape=[jax.ShapeDtypeStruct((4, TR, TC), f32), jax.ShapeDtypeStruct((TILES, 128), f32)],
        in_specs=[whole(pltpu.SMEM)] + [whole()] * 5,
        out_specs=[whole()] * 2,
        compiler_params=params,
    )(place, fields, from_west, from_east, from_north, from_south)
    spread = lax.all_to_all(moments, AXES, split_axis=0, concat_axis=0, tiled=True)
    return pl.pallas_call(
        finish_kernel,
        out_shape=[jax.ShapeDtypeStruct((TR, TC), f32)] * 2,
        in_specs=[whole()] * 2,
        out_specs=[whole()] * 2,
        compiler_params=params,
    )(spread, basis)


def solution(mesh):
    return jax.shard_map(
        body,
        mesh=mesh,
        in_specs=(
            P(AXES, None),
            P(AXES, None),
            P(AXES, None, None),
            P(AXES, None),
            P(AXES, None),
            P(AXES),
        ),
        out_specs=(P("north", "east"), P("north", "east")),
        check_vma=False,
    )
```

```python
import jax
import jax.numpy as jnp
from jax import lax
from jax.experimental import pallas as pl
from jax.experimental.pallas import tpu as pltpu
from jax.sharding import PartitionSpec as P

TR = 128
TC = 128
BLK_DEV = 256
MOST = 4
N_NORTH = 4
N_EAST = 32
TILES = N_NORTH * N_EAST
SHRINK = 1.0 / 64.0
TENSION = 0.75
AXES = ("north", "east")
f32 = jnp.float32
bf16 = jnp.bfloat16

UNITS = 8
GROUPS = TILES * MOST // 128
HALF = 32
WINDOW = 2 * HALF
BANDS = 16
TWO_HOT = 10
LEFT_ROWS = BANDS * HALF + 16
REACH = 192
STEPS = 128 // UNITS
JOIN = 4


def whole(space=pltpu.VMEM):
    return pl.BlockSpec(memory_space=space)


def sort_lanes(keys):
    lane = lax.broadcasted_iota(jnp.int32, keys.shape, 1)
    size = 2
    while size <= 128:
        gap = size // 2
        while gap >= 1:
            low = (lane & gap) == 0
            other = jnp.where(low, pltpu.roll(keys, 128 - gap, 1), pltpu.roll(keys, gap, 1))
            take_min = low == ((lane & size) == 0)
            keys = jnp.where(take_min, jnp.minimum(keys, other), jnp.maximum(keys, other))
            gap //= 2
        size *= 2
    return keys


SORT_ROWS = 256


def route_kernel(dest_ref, count_ref, cells_ref, frac_ref, weight_ref, height_ref, out_ref, seen_ref, sorted_ref):
    out_ref[...] = jnp.zeros_like(out_ref)

    def clear(k, _):
        seen_ref[k] = 0
        return 0

    lax.fori_loop(0, TILES, clear, 0, unroll=8)

    def arrange(part, _):
        rows = pl.ds(part * SORT_ROWS, SORT_ROWS)
        cell = cells_ref[rows, :].astype(f32)
        lane = lax.broadcasted_iota(jnp.int32, cell.shape, 1).astype(f32)
        keys = sort_lanes(jnp.floor((cell + 0.5) * (1.0 / 127.0)) * 128.0 + lane)
        source = (keys - 128.0 * jnp.floor(keys * (1.0 / 128.0))).astype(jnp.int32)
        values = [cell, frac_ref[rows, 0, :], frac_ref[rows, 1, :], weight_ref[rows, :], height_ref[rows, :]]
        for f, v in enumerate(values):
            sorted_ref[f, rows, :] = jnp.take_along_axis(v, source, axis=1)
        return 0

    lax.fori_loop(0, BLK_DEV // SORT_ROWS, arrange, 0)

    def place(b, _):
        tile = dest_ref[b]
        rank = seen_ref[tile]
        seen_ref[tile] = rank + 1
        for f in range(5):
            out_ref[tile, f, pl.ds(rank, 1), :] = sorted_ref[f, pl.ds(b, 1), :]
        return 0

    lax.fori_loop(0, count_ref[0], place, 0)


def high_low(value):
    high = value.astype(bf16).astype(f32)
    return [high, value - high]


def row_of(cell):
    return jnp.floor((cell + 0.5) * (1.0 / 127.0))


def build(rank, base, group, by_rank_ref, vals_ref):
    lanes_in = slice(group * 128, group * 128 + 128)
    cell, d, e, mass, height = [by_rank_ref[f, pl.ds(rank, UNITS), lanes_in] for f in range(5)]
    i = row_of(cell)
    j = cell - 127.0 * i
    inner = i - base.astype(f32)
    lower = inner >= float(HALF)
    i_in = jnp.where((inner >= 0.0) & (inner < float(WINDOW)), jnp.where(lower, inner - float(HALF), inner), -100.0)
    place = j + jnp.where(lower, 128.0, 0.0)
    a0, a1, b0, b1 = 1.0 - d, d, 1.0 - e, e
    mh = mass * height
    cols = [mass * b0 * b0, mass * b1 * b1, mass * b0 * b1]
    ends = [mh * b0, mh * b1]
    down, up, mid = [], [], []
    for c in cols:
        down += high_low(c * a1 * a1)
        up += high_low(c * a0 * a0)
        mid += high_low(c * a0 * a1)
    for c in ends:
        down += high_low(c * a1)
        up += high_low(c * a0)
    for k, v in enumerate(down + up + mid + [i_in, place]):
        vals_ref[group, k * UNITS:(k + 1) * UNITS, :] = v
    iota = lax.broadcasted_iota(jnp.int32, (16, 128), 0).astype(f32).astype(bf16)
    zero = jnp.zeros((16, 128), bf16)
    one = jnp.ones((16, 128), bf16)

    def row(k, s):
        return jnp.broadcast_to(vals_ref[group, k * UNITS + s:k * UNITS + s + 1, :], (16, 128))

    lefts, rights = [], []
    for s in range(UNITS):
        i_row = row(26, s)
        i_b = i_row.astype(bf16)
        i_next = (i_row + 1.0).astype(bf16)
        at = [(iota + float(16 * g)) == i_b for g in range(HALF // 16)]
        after = [(iota + float(16 * g)) == i_next for g in range(HALF // 16)]
        pieces = []
        for k in range(TWO_HOT):
            v1 = row(k, s).astype(bf16)
            v0 = row(TWO_HOT + k, s).astype(bf16)
            for g in range(HALF // 16):
                pieces.append(jnp.where(at[g], v0, jnp.where(after[g], v1, zero)))
        for k in range(BANDS - TWO_HOT):
            v = row(2 * TWO_HOT + k, s).astype(bf16)
            for g in range(HALF // 16):
                pieces.append(jnp.where(at[g], v, zero))
        spill = vals_ref[group, pl.ds(s, 16, stride=UNITS), :]
        pieces.append(jnp.where(i_row == float(HALF - 1), spill, 0.0).astype(bf16))
        lefts.append(jnp.concatenate(pieces, axis=0))
        p_b = row(27, s).astype(bf16)
        rights.append(jnp.concatenate([jnp.where((iota + float(16 * g)) == p_b, one, zero) for g in range(16)], axis=0))
    return lefts, rights


def shifted(a, by, axis):
    return pltpu.roll(a, by % a.shape[axis], axis)


def gather_kernel(x_ref, fields_ref, top_ref, bottom_ref, west_ref, east_ref,
                  by_rank_ref, bounds_ref, limits_ref, items_ref, vals_ref,
                  acc_ref, sem):
    low = []
    high = []
    for g in range(GROUPS):
        lanes = slice(g * 128, g * 128 + 128)
        for f in range(5):
            by_rank_ref[f, :, lanes] = x_ref[g * 32:g * 32 + 32, f].reshape(128, 128).T
        i = row_of(by_rank_ref[0, :, lanes])
        live = by_rank_ref[3, :, lanes] > 0.0
        low.append(jnp.where(live, i, 1000.0))
        high.append(jnp.where(live, i, -1.0))
    least, most = low[0], high[0]
    for g in range(1, GROUPS):
        least = jnp.minimum(least, low[g])
        most = jnp.maximum(most, high[g])
    bounds_ref[0:8, :] = jnp.broadcast_to(jnp.min(least.T, axis=0, keepdims=True), (8, 128)).astype(jnp.int32)
    bounds_ref[8:16, :] = jnp.broadcast_to(jnp.max(most.T, axis=0, keepdims=True), (8, 128)).astype(jnp.int32)
    copy = pltpu.make_async_copy(bounds_ref, limits_ref, sem)
    copy.start()
    acc_ref[...] = jnp.zeros_like(acc_ref)
    copy.wait()

    count = jnp.int32(0)
    for q in range(STEPS):
        first = limits_ref[0, q * UNITS]
        last = limits_ref[8, q * UNITS + UNITS - 1]
        base = (first // 8) * 8
        for w in range(2):
            items_ref[0, count] = q * UNITS
            items_ref[1, count] = base + w * WINDOW
            count = count + (base + w * WINDOW <= last).astype(jnp.int32)
    for extra in range(2):
        items_ref[0, count + extra] = 0
        items_ref[1, count + extra] = 1000

    sub = lax.broadcasted_iota(jnp.int32, (8, 128), 0)

    def step(t, _):
        rank = pl.multiple_of(items_ref[0, t], UNITS)
        base = pl.multiple_of(items_ref[1, t], 8)
        out = None
        for part in range(GROUPS // JOIN):
            lefts, rights = [], []
            for g in range(part * JOIN, part * JOIN + JOIN):
                more = build(rank, base, g, by_rank_ref, vals_ref)
                lefts += more[0]
                rights += more[1]
            piece = lax.dot_general(
                jnp.concatenate(lefts, axis=1), jnp.concatenate(rights, axis=1),
                (((1,), (1,)), ((), ())), preferred_element_type=f32)
            out = piece if out is None else out + piece
        for k in range(BANDS):
            for h in range(2):
                rows = pl.ds(k * REACH + base + h * HALF, HALF)
                acc_ref[rows, :] += out[k * HALF:(k + 1) * HALF, h * 128:(h + 1) * 128]
        for k in range(TWO_HOT):
            for h in range(2):
                rows = pl.ds(k * REACH + base + (h + 1) * HALF, 8)
                line = BANDS * HALF + k
                acc_ref[rows, :] += jnp.where(sub == 0, out[line:line + 1, h * 128:(h + 1) * 128], 0.0)

        return 0

    lax.fori_loop(0, count, step, 0)

    def band(k):
        return acc_ref[k * REACH:k * REACH + TR, :]

    def pair(k):
        return band(k) + band(k + 1)

    diag = pair(0) + shifted(pair(2), 1, 1)
    along_east = pair(4)
    rhs = pair(6) + shifted(pair(8), 1, 1)
    along_south = pair(10) + shifted(pair(12), 1, 1)
    cross = pair(14)
    for k, v in enumerate([rhs, diag, along_east, along_south, cross]):
        fields_ref[k] = v
        top_ref[k] = v[0:8]
        bottom_ref[k] = v[120:128]
        t = v.T
        west_ref[k] = t[0:8]
        east_ref[k] = t[120:128]


def corner_kernel(top_ref, bottom_ref, from_west_ref, from_east_ref, north_ref, south_ref):
    lane = lax.broadcasted_iota(jnp.int32, (8, 128), 1)
    for k in range(5):
        w = from_west_ref[k]
        e = shifted(from_east_ref[k], 64, 1)
        north_ref[k] = top_ref[k]
        south_ref[k] = bottom_ref[k]
        north_ref[5 + k] = jnp.where(lane < 64, w, e)
        south_ref[5 + k] = jnp.where(lane >= 64, w, e)


EXT_R = 144
EXT_C = 256


def krylov_kernel(place_ref, fields_ref, from_west_ref, from_east_ref, from_north_ref, from_south_ref,
                  basis_ref, moments_ref):
    gn = place_ref[0]
    ge = place_ref[1]
    rows = lax.broadcasted_iota(jnp.int32, (EXT_R, EXT_C), 0)
    cols = lax.broadcasted_iota(jnp.int32, (EXT_R, EXT_C), 1)
    grow = gn * TR + jnp.where(rows < 136, rows, rows - EXT_R)
    gcol = ge * TC + jnp.where(cols < 192, cols, cols - EXT_C)
    inside = (grow >= 0) & (grow < N_NORTH * TR) & (gcol >= 0) & (gcol < N_EAST * TC)

    ext = []
    for k in range(5):
        w = from_west_ref[k]
        e = from_east_ref[k]
        n = from_north_ref[5 + k]
        s = from_south_ref[5 + k]
        zeros = jnp.zeros((112, 128), f32)
        side = jnp.concatenate([e, zeros, w], axis=0).T
        n_e = shifted(n, 64, 1)
        s_e = shifted(s, 64, 1)
        south_side = jnp.concatenate([s_e, zeros, s], axis=0).T
        north_side = jnp.concatenate([n_e, zeros, n], axis=0).T
        left = jnp.concatenate([fields_ref[k], from_south_ref[k], from_north_ref[k]], axis=0)
        right = jnp.concatenate([side, south_side[0:8], north_side[120:128]], axis=0)
        full = jnp.concatenate([left, right], axis=1)
        ext.append(jnp.where(inside, full, 0.0))
    v0, diag, along_east, along_south, cross = ext

    def laplace(u, u_l, u_r, u_u, u_d):
        return jnp.where(inside, u_l + u_r + u_u + u_d - 4.0 * u, 0.0)

    def operate(u):
        u_r = shifted(u, -1, 1)
        u_l = shifted(u, 1, 1)
        u_d = shifted(u, -1, 0)
        u_u = shifted(u, 1, 0)
        lu = laplace(u, u_l, u_r, u_u, u_d)
        llu = laplace(lu, shifted(lu, 1, 1), shifted(lu, -1, 1), shifted(lu, 1, 0), shifted(lu, -1, 0))
        u_rd = shifted(u_r, -1, 0)
        out = diag * u + along_east * u_r + along_south * u_d + cross * u_rd
        out = out + shifted(along_east * u + cross * u_d, 1, 1)
        out = out + shifted(along_south * u + cross * u_r + shifted(cross * u, 1, 1), 1, 0)
        return (out + (1.0 - TENSION) * llu - TENSION * lu) * SHRINK

    v = [v0]
    for _ in range(3):
        v.append(operate(v[-1]))
    own = [a[0:TR, 0:TC] for a in v]
    for k in range(4):
        basis_ref[k] = own[k]
    pairs = [(0, 0), (0, 1), (1, 1), (1, 2), (2, 2), (2, 3)]
    lane = lax.broadcasted_iota(jnp.int32, (TILES, 128), 1)
    out = jnp.zeros((TILES, 128), f32)
    for k, (p, q) in enumerate(pairs):
        m = jnp.sum(jnp.sum(own[p] * own[q], axis=0, keepdims=True), axis=1, keepdims=True)
        out = jnp.where(lane == k, m, out)
    moments_ref[...] = out


def finish_kernel(moments_ref, basis_ref, surface_ref, residual_ref):
    total = jnp.sum(moments_ref[...], axis=0, keepdims=True)
    m = [total[:, k:k + 1] for k in range(6)]

    def dot(p, q, shift):
        terms = [p[a] * q[b] * m[a + b + shift] for a in range(len(p)) for b in range(len(q))]
        s = terms[0]
        for t in terms[1:]:
            s = s + t
        return s

    one = jnp.ones_like(m[0])
    res = [one]
    direction = [one]
    surf = []
    rr = m[0]
    for it in range(3):
        alpha = rr / dot(direction, direction, 1)
        surf = [(surf[k] if k < len(surf) else 0.0) + alpha * direction[k] for k in range(len(direction))]
        stepped = [jnp.zeros_like(one)] + [alpha * c for c in direction]
        res = [(res[k] if k < len(res) else 0.0) - stepped[k] for k in range(len(stepped))]
        if it < 2:
            fresh = dot(res, res, 0)
            beta = fresh / rr
            direction = [res[k] + (beta * direction[k] if k < len(direction) else 0.0) for k in range(len(res))]
            rr = fresh
    basis = [basis_ref[k] for k in range(4)]
    out = (surf[0] * SHRINK) * basis[0]
    for k in range(1, 3):
        out = out + (surf[k] * SHRINK) * basis[k]
    surface_ref[...] = out
    out = res[0] * basis[0]
    for k in range(1, 4):
        out = out + res[k] * basis[k]
    residual_ref[...] = out


def body(destinations, cells, fractions, weights, heights, counts):
    params = pltpu.CompilerParams(vmem_limit_bytes=40 * 1024 * 1024)
    send = pl.pallas_call(
        route_kernel,
        out_shape=jax.ShapeDtypeStruct((TILES, 5, MOST, 128), f32),
        in_specs=[whole(pltpu.SMEM), whole(pltpu.SMEM)] + [whole()] * 4,
        out_specs=whole(),
        scratch_shapes=[pltpu.SMEM((TILES,), jnp.int32), pltpu.VMEM((5, BLK_DEV, 128), f32)],
        compiler_params=params,
    )(destinations.reshape(BLK_DEV), counts, cells, fractions, weights, heights)
    got = lax.all_to_all(send, AXES, split_axis=0, concat_axis=0, tiled=True)
    strip = jax.ShapeDtypeStruct((5, 8, 128), f32)
    fields, top, bottom, west, east = pl.pallas_call(
        gather_kernel,
        out_shape=[jax.ShapeDtypeStruct((5, TR, TC), f32)] + [strip] * 4,
        in_specs=[whole()],
        out_specs=[whole()] * 5,
        scratch_shapes=[
            pltpu.VMEM((5, 128, GROUPS * 128), f32),
            pltpu.VMEM((16, 128), jnp.int32),
            pltpu.SMEM((16, 128), jnp.int32),
            pltpu.SMEM((2, 2 * STEPS + 8), jnp.int32),
            pltpu.VMEM((GROUPS, 28 * UNITS, 128), f32),
            pltpu.VMEM((BANDS * REACH, 128), f32),
            pltpu.SemaphoreType.DMA,
        ],
        compiler_params=params,
    )(got)
    up_e = [(i, (i + 1) % N_EAST) for i in range(N_EAST)]
    down_e = [(j, i) for i, j in up_e]
    up_n = [(i, (i + 1) % N_NORTH) for i in range(N_NORTH)]
    down_n = [(j, i) for i, j in up_n]
    from_west = lax.ppermute(east, "east", up_e)
    from_east = lax.ppermute(west, "east", down_e)
    message = jax.ShapeDtypeStruct((10, 8, 128), f32)
    to_north, to_south = pl.pallas_call(
        corner_kernel,
        out_shape=[message] * 2,
        in_specs=[whole()] * 4,
        out_specs=[whole()] * 2,
        compiler_params=params,
    )(top, bottom, from_west, from_east)
    from_north = lax.ppermute(to_south, "north", up_n)
    from_south = lax.ppermute(to_north, "north", down_n)
    place = jnp.stack([lax.axis_index("north"), lax.axis_index("east")]).astype(jnp.int32)
    basis, moments = pl.pallas_call(
        krylov_kernel,
        out_shape=[jax.ShapeDtypeStruct((4, TR, TC), f32), jax.ShapeDtypeStruct((TILES, 128), f32)],
        in_specs=[whole(pltpu.SMEM)] + [whole()] * 5,
        out_specs=[whole()] * 2,
        compiler_params=params,
    )(place, fields, from_west, from_east, from_north, from_south)
    spread = lax.all_to_all(moments, AXES, split_axis=0, concat_axis=0, tiled=True)
    return pl.pallas_call(
        finish_kernel,
        out_shape=[jax.ShapeDtypeStruct((TR, TC), f32)] * 2,
        in_specs=[whole()] * 2,
        out_specs=[whole()] * 2,
        compiler_params=params,
    )(spread, basis)


def solution(mesh):
    return jax.shard_map(
        body,
        mesh=mesh,
        in_specs=(
            P(AXES, None),
            P(AXES, None),
            P(AXES, None, None),
            P(AXES, None),
            P(AXES, None),
            P(AXES),
        ),
        out_specs=(P("north", "east"), P("north", "east")),
        check_vma=False,
    )
```

```python
import jax
import jax.numpy as jnp
from jax import lax
from jax.experimental import pallas as pl
from jax.experimental.pallas import tpu as pltpu
from jax.sharding import PartitionSpec as P

TR = 128
TC = 128
BLK_DEV = 256
MOST = 4
N_NORTH = 4
N_EAST = 32
TILES = N_NORTH * N_EAST
SHRINK = 1.0 / 64.0
TENSION = 0.75
AXES = ("north", "east")
f32 = jnp.float32
bf16 = jnp.bfloat16

UNITS = 8
GROUPS = TILES * MOST // 128
PAIRS = GROUPS // 2
HALF = 24
WINDOW = 2 * HALF
BANDS = 16
TWO_HOT = 10
SPILL = BANDS * HALF
REACH = 176
STEPS = 128 // UNITS
WINDOWS = -(-127 // WINDOW)


def whole(space=pltpu.VMEM):
    return pl.BlockSpec(memory_space=space)


def row_of(cell):
    return jnp.floor((cell + 0.5) * (1.0 / 127.0))


def sort_lanes(keys):
    lane = lax.broadcasted_iota(jnp.int32, keys.shape, 1)
    size = 2
    while size <= 128:
        gap = size // 2
        while gap >= 1:
            low = (lane & gap) == 0
            other = jnp.take_along_axis(keys, lane ^ gap, axis=1)
            take_min = low == ((lane & size) == 0)
            keys = jnp.where(take_min, jnp.minimum(keys, other), jnp.maximum(keys, other))
            gap //= 2
        size *= 2
    return keys


def route_kernel(dest_hbm, count_ref, cells_hbm, frac_hbm, weight_hbm, height_hbm, out_ref,
                 dest_ref, seen_ref, slot_ref, cells_ref, frac_ref, weight_ref, height_ref, sorted_ref, sems):
    copies = [
        pltpu.make_async_copy(src, dst, sems.at[k])
        for k, (src, dst) in enumerate([
            (dest_hbm, dest_ref), (cells_hbm, cells_ref), (frac_hbm, frac_ref),
            (weight_hbm, weight_ref), (height_hbm, height_ref)])
    ]
    for c in copies:
        c.start()

    def clear(k, _):
        seen_ref[k] = 0
        out_ref[k, 3] = jnp.zeros((MOST, 128), f32)
        return 0

    lax.fori_loop(0, TILES, clear, 0, unroll=8)
    for c in copies:
        c.wait()
    for b in range(BLK_DEV):
        tile = dest_ref[b]
        rank = seen_ref[tile]
        seen_ref[tile] = rank + 1
        slot_ref[b] = rank
    cell = cells_ref[...].astype(f32)
    lane = lax.broadcasted_iota(jnp.int32, cell.shape, 1).astype(f32)
    keys = sort_lanes(row_of(cell) * 128.0 + lane)
    source = (keys - 128.0 * jnp.floor(keys * (1.0 / 128.0))).astype(jnp.int32)
    live = lax.broadcasted_iota(jnp.int32, cell.shape, 0) < count_ref[0]
    weight = jnp.where(live, weight_ref[...], 0.0)
    values = [cell, frac_ref[:, 0, :], frac_ref[:, 1, :], weight, height_ref[...]]
    for f, v in enumerate(values):
        sorted_ref[f] = jnp.take_along_axis(v, source, axis=1)

    for b in range(BLK_DEV):
        tile = dest_ref[b]
        rank = slot_ref[b]
        for f in range(5):
            out_ref[tile, f, pl.ds(rank, 1), :] = sorted_ref[f, b:b + 1, :]


def high_low(value):
    high = value.astype(bf16).astype(f32)
    return [high, value - high]


def build(rank, base, pair, group, by_rank_ref, vals_ref):
    lanes_in = slice(group * 128, group * 128 + 128)
    cell, d, e, mass, height = [by_rank_ref[pair, f, pl.ds(rank, UNITS), lanes_in] for f in range(5)]
    i = row_of(cell)
    j = cell - 127.0 * i
    inner = i - base.astype(f32)
    lower = inner >= float(HALF)
    i_in = jnp.where((inner >= 0.0) & (inner < float(WINDOW)), jnp.where(lower, inner - float(HALF), inner), -100.0)
    place = j + jnp.where(lower, 128.0, 0.0)
    a0, a1, b0, b1 = 1.0 - d, d, 1.0 - e, e
    mh = mass * height
    cols = [mass * b0 * b0, mass * b1 * b1, mass * b0 * b1]
    ends = [mh * b0, mh * b1]
    down, up, mid = [], [], []
    for c in cols:
        down += high_low(c * a1 * a1)
        up += high_low(c * a0 * a0)
        mid += high_low(c * a0 * a1)
    for c in ends:
        down += high_low(c * a1)
        up += high_low(c * a0)
    for k, v in enumerate(down + up + mid + [i_in, place]):
        vals_ref[group, k * UNITS:(k + 1) * UNITS, :] = v
    iota = lax.broadcasted_iota(jnp.int32, (16, 128), 0).astype(f32).astype(bf16)
    zero = jnp.zeros((16, 128), bf16)
    one = jnp.ones((16, 128), bf16)

    def row(k, s):
        return jnp.broadcast_to(vals_ref[group, k * UNITS + s:k * UNITS + s + 1, :], (16, 128))

    eighth = jnp.where(iota < 8.0, iota, iota - 8.0) + 16.0
    first = iota < 8.0
    lefts, rights = [], []
    for s in range(UNITS):
        i_row = row(26, s)
        i_b = i_row.astype(bf16)
        i_next = (i_row + 1.0).astype(bf16)
        at, at_end = iota == i_b, eighth == i_b
        after, after_end = iota == i_next, eighth == i_next
        pieces = []
        for k in range(0, TWO_HOT, 2):
            v1 = [row(k + n, s).astype(bf16) for n in range(2)]
            v0 = [row(TWO_HOT + k + n, s).astype(bf16) for n in range(2)]
            for n in range(2):
                pieces.append(jnp.where(at, v0[n], jnp.where(after, v1[n], zero)))
            pieces.append(jnp.where(at_end, jnp.where(first, v0[0], v0[1]),
                                    jnp.where(after_end, jnp.where(first, v1[0], v1[1]), zero)))
        for k in range(2 * TWO_HOT, 2 * TWO_HOT + BANDS - TWO_HOT, 2):
            v = [row(k + n, s).astype(bf16) for n in range(2)]
            for n in range(2):
                pieces.append(jnp.where(at, v[n], zero))
            pieces.append(jnp.where(at_end, jnp.where(first, v[0], v[1]), zero))
        spill = vals_ref[group, pl.ds(s, 16, stride=UNITS), :]
        pieces.append(jnp.where(i_row == float(HALF - 1), spill, 0.0).astype(bf16))
        lefts.append(jnp.concatenate(pieces, axis=0))
        p_b = row(27, s).astype(bf16)
        rights.append(jnp.concatenate([jnp.where((iota + float(16 * g)) == p_b, one, zero) for g in range(16)], axis=0))
    return lefts, rights


def shifted(a, by, axis):
    return pltpu.roll(a, by % a.shape[axis], axis)


def gather_kernel(place_ref, x_ref, fields_ref, top_ref, bottom_ref, across_ref, beside_ref,
                  by_rank_ref, bounds_ref, limits_ref, items_ref, vals_ref, acc_ref, sem):
    for p in range(PAIRS):
        least, most = [], []
        for g in range(2):
            lanes = slice(g * 128, g * 128 + 128)
            first = (2 * p + g) * 32
            fields = [x_ref[first:first + 32, f].reshape(128, 128).T for f in range(5)]
            live = fields[3] > 0.0
            fields = [jnp.where(live, v, 0.0) for v in fields]
            for f, v in enumerate(fields):
                by_rank_ref[p, f, :, lanes] = v
            i = row_of(fields[0])
            least.append(jnp.where(live, i, 1000.0))
            most.append(jnp.where(live, i, -1.0))
        low = jnp.min(jnp.minimum(least[0], least[1]).T, axis=0, keepdims=True)
        high = jnp.max(jnp.maximum(most[0], most[1]).T, axis=0, keepdims=True)
        bounds_ref[16 * p:16 * p + 8, :] = jnp.broadcast_to(low, (8, 128)).astype(jnp.int32)
        bounds_ref[16 * p + 8:16 * p + 16, :] = jnp.broadcast_to(high, (8, 128)).astype(jnp.int32)
    copy = pltpu.make_async_copy(bounds_ref, limits_ref, sem)
    copy.start()
    acc_ref[...] = jnp.zeros_like(acc_ref)
    copy.wait()

    count = jnp.int32(0)
    for q in range(STEPS):
        for p in range(PAIRS):
            first = limits_ref[16 * p, q * UNITS]
            last = limits_ref[16 * p + 8, q * UNITS + UNITS - 1]
            base = (first // 8) * 8
            for w in range(WINDOWS):
                items_ref[0, count] = q * UNITS
                items_ref[1, count] = base + w * WINDOW
                items_ref[2, count] = p
                count = count + (base + w * WINDOW <= last).astype(jnp.int32)
    items_ref[0, count] = 0
    items_ref[1, count] = 1000
    items_ref[2, count] = 0

    sub = lax.broadcasted_iota(jnp.int32, (8, 128), 0)

    def item(t, half):
        rank = pl.multiple_of(items_ref[0, t], UNITS)
        base = items_ref[1, t]
        lefts, rights = [], []
        for g in range(2):
            more = build(rank, base, items_ref[2, t], g, by_rank_ref, vals_ref.at[half])
            lefts += more[0]
            rights += more[1]
        out = lax.dot_general(
            jnp.concatenate(lefts, axis=1), jnp.concatenate(rights, axis=1),
            (((1,), (1,)), ((), ())), preferred_element_type=f32)
        base = pl.multiple_of(jnp.where(base > 127, 0, base), 8)
        for k in range(0, BANDS, 2):
            for n in range(2):
                for h in range(2):
                    start = (k + n) * REACH + base + h * HALF
                    cols = slice(h * 128, h * 128 + 128)
                    line = k * HALF + 16 * n
                    acc_ref[pl.ds(start, 16), :] += out[line:line + 16, cols]
                    line = k * HALF + 32 + 8 * n
                    acc_ref[pl.ds(start + 16, 8), :] += out[line:line + 8, cols]
        for k in range(TWO_HOT):
            for h in range(2):
                rows = pl.ds(k * REACH + base + (h + 1) * HALF, 8)
                acc_ref[rows, :] += jnp.where(sub == 0, out[SPILL + k:SPILL + k + 1, h * 128:(h + 1) * 128], 0.0)

    def step(c, _):
        item(2 * c, 0)
        item(2 * c + 1, 1)
        return 0

    lax.fori_loop(0, (count + 1) // 2, step, 0)

    def band(k):
        return acc_ref[k * REACH:k * REACH + TR, :]

    def pair(k):
        return band(k) + band(k + 1)

    diag = pair(0) + shifted(pair(2), 1, 1)
    along_east = pair(4)
    rhs = pair(6) + shifted(pair(8), 1, 1)
    along_south = pair(10) + shifted(pair(12), 1, 1)
    cross = pair(14)
    even = place_ref[1] % 2 == 0
    for k, v in enumerate([rhs, diag, along_east, along_south, cross]):
        fields_ref[k] = v
        top_ref[k] = v[0:8]
        bottom_ref[k] = v[120:128]
        t = v.T
        west, east = t[0:8], t[120:128]
        across_ref[k] = jnp.where(even, east, west)
        beside_ref[k] = jnp.where(even, west, east)


def corner_kernel(place_ref, top_ref, bottom_ref, across_ref, beside_ref, to_across_ref, to_beside_ref):
    lane = lax.broadcasted_iota(jnp.int32, (8, 128), 1)
    even_north = place_ref[0] % 2 == 0
    even_east = place_ref[1] % 2 == 0
    for k in range(5):
        a, b = across_ref[k], beside_ref[k]
        w = jnp.where(even_east, b, a)
        e = shifted(jnp.where(even_east, a, b), 64, 1)
        north = jnp.where(lane < 64, w, e)
        south = jnp.where(lane >= 64, w, e)
        top, bottom = top_ref[k], bottom_ref[k]
        to_across_ref[k] = jnp.where(even_north, bottom, top)
        to_beside_ref[k] = jnp.where(even_north, top, bottom)
        to_across_ref[5 + k] = jnp.where(even_north, south, north)
        to_beside_ref[5 + k] = jnp.where(even_north, north, south)


EXT_R = 144
EXT_C = 256


def krylov_kernel(place_ref, fields_ref, across_e_ref, beside_e_ref, across_n_ref, beside_n_ref,
                  basis_ref, moments_ref):
    gn = place_ref[0]
    ge = place_ref[1]
    rows = lax.broadcasted_iota(jnp.int32, (EXT_R, EXT_C), 0)
    cols = lax.broadcasted_iota(jnp.int32, (EXT_R, EXT_C), 1)
    grow = gn * TR + jnp.where(rows < 136, rows, rows - EXT_R)
    gcol = ge * TC + jnp.where(cols < 192, cols, cols - EXT_C)
    inside = (grow >= 0) & (grow < N_NORTH * TR) & (gcol >= 0) & (gcol < N_EAST * TC)

    even_north = gn % 2 == 0
    even_east = ge % 2 == 0
    ext = []
    for k in range(5):
        a, b = across_e_ref[k], beside_e_ref[k]
        w, e = jnp.where(even_east, b, a), jnp.where(even_east, a, b)
        a, b = across_n_ref[k], beside_n_ref[k]
        from_north, from_south = jnp.where(even_north, b, a), jnp.where(even_north, a, b)
        a, b = across_n_ref[5 + k], beside_n_ref[5 + k]
        n, s = jnp.where(even_north, b, a), jnp.where(even_north, a, b)
        zeros = jnp.zeros((112, 128), f32)
        side = jnp.concatenate([e, zeros, w], axis=0).T
        n_e = shifted(n, 64, 1)
        s_e = shifted(s, 64, 1)
        south_side = jnp.concatenate([s_e, zeros, s], axis=0).T
        north_side = jnp.concatenate([n_e, zeros, n], axis=0).T
        left = jnp.concatenate([fields_ref[k], from_south, from_north], axis=0)
        right = jnp.concatenate([side, south_side[0:8], north_side[120:128]], axis=0)
        full = jnp.concatenate([left, right], axis=1)
        ext.append(jnp.where(inside, full, 0.0))
    v0, diag, along_east, along_south, cross = ext

    def laplace(u, u_l, u_r, u_u, u_d):
        return jnp.where(inside, u_l + u_r + u_u + u_d - 4.0 * u, 0.0)

    def operate(u):
        u_r = shifted(u, -1, 1)
        u_l = shifted(u, 1, 1)
        u_d = shifted(u, -1, 0)
        u_u = shifted(u, 1, 0)
        lu = laplace(u, u_l, u_r, u_u, u_d)
        llu = laplace(lu, shifted(lu, 1, 1), shifted(lu, -1, 1), shifted(lu, 1, 0), shifted(lu, -1, 0))
        u_rd = shifted(u_r, -1, 0)
        out = diag * u + along_east * u_r + along_south * u_d + cross * u_rd
        out = out + shifted(along_east * u + cross * u_d, 1, 1)
        out = out + shifted(along_south * u + cross * u_r + shifted(cross * u, 1, 1), 1, 0)
        return (out + (1.0 - TENSION) * llu - TENSION * lu) * SHRINK

    v = [v0]
    for _ in range(3):
        v.append(operate(v[-1]))
    own = [a[0:TR, 0:TC] for a in v]
    for k in range(4):
        basis_ref[k] = own[k]
    pairs = [(0, 0), (0, 1), (1, 1), (1, 2), (2, 2), (2, 3)]
    lane = lax.broadcasted_iota(jnp.int32, (TILES, 128), 1)
    out = jnp.zeros((TILES, 128), f32)
    for k, (p, q) in enumerate(pairs):
        m = jnp.sum(jnp.sum(own[p] * own[q], axis=0, keepdims=True), axis=1, keepdims=True)
        out = jnp.where(lane == k, m, out)
    moments_ref[...] = out


def finish_kernel(moments_ref, basis_ref, surface_ref, residual_ref):
    total = jnp.sum(moments_ref[...], axis=0, keepdims=True)
    m = [total[:, k:k + 1] for k in range(6)]

    def dot(p, q, shift):
        terms = [p[a] * q[b] * m[a + b + shift] for a in range(len(p)) for b in range(len(q))]
        s = terms[0]
        for t in terms[1:]:
            s = s + t
        return s

    one = jnp.ones_like(m[0])
    res = [one]
    direction = [one]
    surf = []
    rr = m[0]
    for it in range(3):
        alpha = rr / dot(direction, direction, 1)
        surf = [(surf[k] if k < len(surf) else 0.0) + alpha * direction[k] for k in range(len(direction))]
        stepped = [jnp.zeros_like(one)] + [alpha * c for c in direction]
        res = [(res[k] if k < len(res) else 0.0) - stepped[k] for k in range(len(stepped))]
        if it < 2:
            fresh = dot(res, res, 0)
            beta = fresh / rr
            direction = [res[k] + (beta * direction[k] if k < len(direction) else 0.0) for k in range(len(res))]
            rr = fresh
    basis = [basis_ref[k] for k in range(4)]
    out = (surf[0] * SHRINK) * basis[0]
    for k in range(1, 3):
        out = out + (surf[k] * SHRINK) * basis[k]
    surface_ref[...] = out
    out = res[0] * basis[0]
    for k in range(1, 4):
        out = out + res[k] * basis[k]
    residual_ref[...] = out


def swaps(count):
    across = [(i, i ^ 1) for i in range(count)]
    beside = [(0, 0), (count - 1, count - 1)]
    for i in range(1, count - 1, 2):
        beside += [(i, i + 1), (i + 1, i)]
    return across, sorted(beside)


def body(destinations, cells, fractions, weights, heights, counts):
    params = pltpu.CompilerParams(vmem_limit_bytes=40 * 1024 * 1024)
    place = jnp.stack([lax.axis_index("north"), lax.axis_index("east")]).astype(jnp.int32)
    block = (BLK_DEV, 128)
    send = pl.pallas_call(
        route_kernel,
        out_shape=jax.ShapeDtypeStruct((TILES, 5, MOST, 128), f32),
        in_specs=[whole(pltpu.HBM), whole(pltpu.SMEM)] + [whole(pltpu.HBM)] * 4,
        out_specs=whole(),
        scratch_shapes=[
            pltpu.SMEM((BLK_DEV,), jnp.int32),
            pltpu.SMEM((TILES,), jnp.int32),
            pltpu.SMEM((BLK_DEV,), jnp.int32),
            pltpu.VMEM(block, jnp.int32),
            pltpu.VMEM((BLK_DEV, 2, 128), f32),
            pltpu.VMEM(block, f32),
            pltpu.VMEM(block, f32),
            pltpu.VMEM((5, BLK_DEV, 128), f32),
            pltpu.SemaphoreType.DMA((5,)),
        ],
        compiler_params=pltpu.CompilerParams(vmem_limit_bytes=60 * 1024 * 1024),
    )(destinations.reshape(BLK_DEV), counts, cells, fractions, weights, heights)
    got = lax.all_to_all(send, AXES, split_axis=0, concat_axis=0, tiled=True)
    strip = jax.ShapeDtypeStruct((5, 8, 128), f32)
    fields, top, bottom, across, beside = pl.pallas_call(
        gather_kernel,
        out_shape=[jax.ShapeDtypeStruct((5, TR, TC), f32)] + [strip] * 4,
        in_specs=[whole(pltpu.SMEM), whole()],
        out_specs=[whole()] * 5,
        scratch_shapes=[
            pltpu.VMEM((PAIRS, 5, 128, 256), f32),
            pltpu.VMEM((16 * PAIRS, 128), jnp.int32),
            pltpu.SMEM((16 * PAIRS, 128), jnp.int32),
            pltpu.SMEM((3, PAIRS * STEPS * WINDOWS + 8), jnp.int32),
            pltpu.VMEM((2, 2, 28 * UNITS, 128), f32),
            pltpu.VMEM((BANDS * REACH, 128), f32),
            pltpu.SemaphoreType.DMA,
        ],
        compiler_params=params,
    )(place, got)
    east_across, east_beside = swaps(N_EAST)
    north_across, north_beside = swaps(N_NORTH)
    beside_e = lax.ppermute(beside, "east", east_beside)
    across_e = lax.ppermute(across, "east", east_across)
    message = jax.ShapeDtypeStruct((10, 8, 128), f32)
    to_across, to_beside = pl.pallas_call(
        corner_kernel,
        out_shape=[message] * 2,
        in_specs=[whole(pltpu.SMEM)] + [whole()] * 4,
        out_specs=[whole()] * 2,
        compiler_params=params,
    )(place, top, bottom, across_e, beside_e)
    beside_n = lax.ppermute(to_beside, "north", north_beside)
    across_n = lax.ppermute(to_across, "north", north_across)
    basis, moments = pl.pallas_call(
        krylov_kernel,
        out_shape=[jax.ShapeDtypeStruct((4, TR, TC), f32), jax.ShapeDtypeStruct((TILES, 128), f32)],
        in_specs=[whole(pltpu.SMEM)] + [whole()] * 5,
        out_specs=[whole()] * 2,
        compiler_params=params,
    )(place, fields, across_e, beside_e, across_n, beside_n)
    spread = lax.all_to_all(moments, AXES, split_axis=0, concat_axis=0, tiled=True)
    return pl.pallas_call(
        finish_kernel,
        out_shape=[jax.ShapeDtypeStruct((TR, TC), f32)] * 2,
        in_specs=[whole()] * 2,
        out_specs=[whole()] * 2,
        compiler_params=params,
    )(spread, basis)


def solution(mesh):
    return jax.shard_map(
        body,
        mesh=mesh,
        in_specs=(
            P(AXES, None),
            P(AXES, None),
            P(AXES, None, None),
            P(AXES, None),
            P(AXES, None),
            P(AXES),
        ),
        out_specs=(P("north", "east"), P("north", "east")),
        check_vma=False,
    )
```

```python
import jax
import jax.numpy as jnp
from jax import lax
from jax.experimental import pallas as pl
from jax.experimental.pallas import tpu as pltpu
from jax.sharding import PartitionSpec as P

TR = 128
TC = 128
BLK_DEV = 256
MOST = 4
N_NORTH = 4
N_EAST = 32
TILES = N_NORTH * N_EAST
SHRINK = 1.0 / 64.0
TENSION = 0.75
AXES = ("north", "east")
f32 = jnp.float32
bf16 = jnp.bfloat16

UNITS = 8
GROUPS = TILES * MOST // 128
PAIRS = GROUPS // 2
HALF = 24
WINDOW = 2 * HALF
BANDS = 16
TWO_HOT = 10
SPILL = BANDS * HALF
REACH = 176
STEPS = 128 // UNITS
WINDOWS = -(-127 // WINDOW)


def whole(space=pltpu.VMEM):
    return pl.BlockSpec(memory_space=space)


def row_of(cell):
    return jnp.floor((cell + 0.5) * (1.0 / 127.0))


def sort_lanes(keys):
    lane = lax.broadcasted_iota(jnp.int32, keys.shape, 1)
    size = 2
    while size <= 128:
        gap = size // 2
        while gap >= 1:
            low = (lane & gap) == 0
            other = jnp.take_along_axis(keys, lane ^ gap, axis=1)
            take_min = low == ((lane & size) == 0)
            keys = jnp.where(take_min, jnp.minimum(keys, other), jnp.maximum(keys, other))
            gap //= 2
        size *= 2
    return keys


def route_kernel(dest_hbm, count_ref, cells_hbm, frac_hbm, weight_hbm, height_hbm, out_ref,
                 dest_ref, seen_ref, slot_ref, cells_ref, frac_ref, weight_ref, height_ref, sorted_ref, sems):
    copies = [
        pltpu.make_async_copy(src, dst, sems.at[k])
        for k, (src, dst) in enumerate([
            (dest_hbm, dest_ref), (cells_hbm, cells_ref), (frac_hbm, frac_ref),
            (weight_hbm, weight_ref), (height_hbm, height_ref)])
    ]
    for c in copies:
        c.start()

    def clear(k, _):
        seen_ref[k] = 0
        out_ref[k, 3] = jnp.zeros((MOST, 128), f32)
        return 0

    lax.fori_loop(0, TILES, clear, 0, unroll=8)
    for c in copies[:2]:
        c.wait()
    for b in range(BLK_DEV):
        tile = dest_ref[b]
        rank = seen_ref[tile]
        seen_ref[tile] = rank + 1
        slot_ref[b] = rank
    cell = cells_ref[...].astype(f32)
    lane = lax.broadcasted_iota(jnp.int32, cell.shape, 1).astype(f32)
    keys = sort_lanes(row_of(cell) * 128.0 + lane)
    source = (keys - 128.0 * jnp.floor(keys * (1.0 / 128.0))).astype(jnp.int32)
    for c in copies[2:]:
        c.wait()
    live = lax.broadcasted_iota(jnp.int32, cell.shape, 0) < count_ref[0]
    weight = jnp.where(live, weight_ref[...], 0.0)
    values = [cell, frac_ref[:, 0, :], frac_ref[:, 1, :], weight, height_ref[...]]
    for f, v in enumerate(values):
        sorted_ref[f] = jnp.take_along_axis(v, source, axis=1)

    for b in range(BLK_DEV):
        tile = dest_ref[b]
        rank = slot_ref[b]
        for f in range(5):
            out_ref[tile, f, pl.ds(rank, 1), :] = sorted_ref[f, b:b + 1, :]


def high_low(value):
    high = value.astype(bf16).astype(f32)
    return [high, value - high]


def build(rank, base, pair, group, by_rank_ref, vals_ref):
    lanes_in = slice(group * 128, group * 128 + 128)
    cell, d, e, mass, height = [by_rank_ref[pair, f, pl.ds(rank, UNITS), lanes_in] for f in range(5)]
    i = row_of(cell)
    j = cell - 127.0 * i
    inner = i - base.astype(f32)
    lower = inner >= float(HALF)
    i_in = jnp.where((inner >= 0.0) & (inner < float(WINDOW)), jnp.where(lower, inner - float(HALF), inner), -100.0)
    place = j + jnp.where(lower, 128.0, 0.0)
    a0, a1, b0, b1 = 1.0 - d, d, 1.0 - e, e
    mh = mass * height
    cols = [mass * b0 * b0, mass * b1 * b1, mass * b0 * b1]
    ends = [mh * b0, mh * b1]
    down, up, mid = [], [], []
    for c in cols:
        down += high_low(c * a1 * a1)
        up += high_low(c * a0 * a0)
        mid += high_low(c * a0 * a1)
    for c in ends:
        down += high_low(c * a1)
        up += high_low(c * a0)
    for k, v in enumerate(down + up + mid + [i_in, place]):
        vals_ref[group, k * UNITS:(k + 1) * UNITS, :] = v
    iota = lax.broadcasted_iota(jnp.int32, (16, 128), 0).astype(f32).astype(bf16)
    zero = jnp.zeros((16, 128), bf16)
    one = jnp.ones((16, 128), bf16)

    def row(k, s):
        return jnp.broadcast_to(vals_ref[group, k * UNITS + s:k * UNITS + s + 1, :], (16, 128))

    eighth = jnp.where(iota < 8.0, iota, iota - 8.0) + 16.0
    first = iota < 8.0
    lefts, rights = [], []
    for s in range(UNITS):
        i_row = row(26, s)
        i_b = i_row.astype(bf16)
        i_next = (i_row + 1.0).astype(bf16)
        at, at_end = iota == i_b, eighth == i_b
        after, after_end = iota == i_next, eighth == i_next
        pieces = []
        for k in range(0, TWO_HOT, 2):
            v1 = [row(k + n, s).astype(bf16) for n in range(2)]
            v0 = [row(TWO_HOT + k + n, s).astype(bf16) for n in range(2)]
            for n in range(2):
                pieces.append(jnp.where(at, v0[n], jnp.where(after, v1[n], zero)))
            pieces.append(jnp.where(at_end, jnp.where(first, v0[0], v0[1]),
                                    jnp.where(after_end, jnp.where(first, v1[0], v1[1]), zero)))
        for k in range(2 * TWO_HOT, 2 * TWO_HOT + BANDS - TWO_HOT, 2):
            v = [row(k + n, s).astype(bf16) for n in range(2)]
            for n in range(2):
                pieces.append(jnp.where(at, v[n], zero))
            pieces.append(jnp.where(at_end, jnp.where(first, v[0], v[1]), zero))
        spill = vals_ref[group, pl.ds(s, 16, stride=UNITS), :]
        pieces.append(jnp.where(i_row == float(HALF - 1), spill, 0.0).astype(bf16))
        lefts.append(jnp.concatenate(pieces, axis=0))
        p_b = row(27, s).astype(bf16)
        rights.append(jnp.concatenate([jnp.where((iota + float(16 * g)) == p_b, one, zero) for g in range(16)], axis=0))
    return lefts, rights


def shifted(a, by, axis):
    return pltpu.roll(a, by % a.shape[axis], axis)


def gather_kernel(place_ref, x_ref, fields_ref, top_ref, bottom_ref, across_ref, beside_ref,
                  by_rank_ref, bounds_ref, limits_ref, items_ref, vals_ref, acc_ref, sem):
    for p in range(PAIRS):
        least, most = [], []
        for g in range(2):
            lanes = slice(g * 128, g * 128 + 128)
            first = (2 * p + g) * 32
            fields = [x_ref[first:first + 32, f].reshape(128, 128).T for f in range(5)]
            live = fields[3] > 0.0
            fields = [jnp.where(live, v, 0.0) for v in fields]
            for f, v in enumerate(fields):
                by_rank_ref[p, f, :, lanes] = v
            i = row_of(fields[0])
            least.append(jnp.where(live, i, 1000.0))
            most.append(jnp.where(live, i, -1.0))
        low = jnp.min(jnp.minimum(least[0], least[1]).T, axis=0, keepdims=True)
        high = jnp.max(jnp.maximum(most[0], most[1]).T, axis=0, keepdims=True)
        bounds_ref[16 * p:16 * p + 8, :] = jnp.broadcast_to(low, (8, 128)).astype(jnp.int32)
        bounds_ref[16 * p + 8:16 * p + 16, :] = jnp.broadcast_to(high, (8, 128)).astype(jnp.int32)
    copy = pltpu.make_async_copy(bounds_ref, limits_ref, sem)
    copy.start()
    acc_ref[...] = jnp.zeros_like(acc_ref)
    copy.wait()

    count = jnp.int32(0)
    for q in range(STEPS):
        for p in range(PAIRS):
            first = limits_ref[16 * p, q * UNITS]
            last = limits_ref[16 * p + 8, q * UNITS + UNITS - 1]
            base = (first // 8) * 8
            for w in range(WINDOWS):
                items_ref[0, count] = q * UNITS
                items_ref[1, count] = base + w * WINDOW
                items_ref[2, count] = p
                count = count + (base + w * WINDOW <= last).astype(jnp.int32)
    items_ref[0, count] = 0
    items_ref[1, count] = 1000
    items_ref[2, count] = 0

    sub = lax.broadcasted_iota(jnp.int32, (8, 128), 0)

    def item(t, half):
        rank = pl.multiple_of(items_ref[0, t], UNITS)
        base = items_ref[1, t]
        lefts, rights = [], []
        for g in range(2):
            more = build(rank, base, items_ref[2, t], g, by_rank_ref, vals_ref.at[half])
            lefts += more[0]
            rights += more[1]
        out = lax.dot_general(
            jnp.concatenate(lefts, axis=1), jnp.concatenate(rights, axis=1),
            (((1,), (1,)), ((), ())), preferred_element_type=f32)
        base = pl.multiple_of(jnp.where(base > 127, 0, base), 8)
        for k in range(0, BANDS, 2):
            for n in range(2):
                for h in range(2):
                    start = (k + n) * REACH + base + h * HALF
                    cols = slice(h * 128, h * 128 + 128)
                    line = k * HALF + 16 * n
                    acc_ref[pl.ds(start, 16), :] += out[line:line + 16, cols]
                    line = k * HALF + 32 + 8 * n
                    acc_ref[pl.ds(start + 16, 8), :] += out[line:line + 8, cols]
        for k in range(TWO_HOT):
            for h in range(2):
                rows = pl.ds(k * REACH + base + (h + 1) * HALF, 8)
                acc_ref[rows, :] += jnp.where(sub == 0, out[SPILL + k:SPILL + k + 1, h * 128:(h + 1) * 128], 0.0)

    def four(c, _):
        for n in range(8):
            item(8 * c + n, n)
        return 0

    def two(c, _):
        for n in range(2):
            item(2 * c + n, n)
        return 0

    lax.fori_loop(0, count // 8, four, 0)
    lax.fori_loop(4 * (count // 8), (count + 1) // 2, two, 0)

    def band(k):
        return acc_ref[k * REACH:k * REACH + TR, :]

    def pair(k):
        return band(k) + band(k + 1)

    diag = pair(0) + shifted(pair(2), 1, 1)
    along_east = pair(4)
    rhs = pair(6) + shifted(pair(8), 1, 1)
    along_south = pair(10) + shifted(pair(12), 1, 1)
    cross = pair(14)
    even = (place_ref[8:16, :] & 1) == 0
    for k, v in enumerate([rhs, diag, along_east, along_south, cross]):
        fields_ref[k] = v
        top_ref[k] = v[0:8]
        bottom_ref[k] = v[120:128]
        t = v.T
        west, east = t[0:8], t[120:128]
        across_ref[k] = jnp.where(even, east, west)
        beside_ref[k] = jnp.where(even, west, east)


def corner_kernel(place_ref, top_ref, bottom_ref, across_ref, beside_ref, to_across_ref, to_beside_ref):
    lane = lax.broadcasted_iota(jnp.int32, (8, 128), 1)
    even_north = (place_ref[0:8, :] & 1) == 0
    even_east = (place_ref[8:16, :] & 1) == 0
    for k in range(5):
        a, b = across_ref[k], beside_ref[k]
        w = jnp.where(even_east, b, a)
        e = shifted(jnp.where(even_east, a, b), 64, 1)
        north = jnp.where(lane < 64, w, e)
        south = jnp.where(lane >= 64, w, e)
        top, bottom = top_ref[k], bottom_ref[k]
        to_across_ref[k] = jnp.where(even_north, bottom, top)
        to_beside_ref[k] = jnp.where(even_north, top, bottom)
        to_across_ref[5 + k] = jnp.where(even_north, south, north)
        to_beside_ref[5 + k] = jnp.where(even_north, north, south)


EXT_R = 144
EXT_C = 256


def krylov_kernel(place_ref, fields_ref, across_e_ref, beside_e_ref, across_n_ref, beside_n_ref,
                  basis_ref, moments_ref):
    north, east = place_ref[0:8, :], place_ref[8:16, :]
    gn = jnp.concatenate([jnp.concatenate([north] * (EXT_R // 8), axis=0)] * 2, axis=1)
    ge = jnp.concatenate([jnp.concatenate([east] * (EXT_R // 8), axis=0)] * 2, axis=1)
    rows = lax.broadcasted_iota(jnp.int32, (EXT_R, EXT_C), 0)
    cols = lax.broadcasted_iota(jnp.int32, (EXT_R, EXT_C), 1)
    grow = gn * TR + jnp.where(rows < 136, rows, rows - EXT_R)
    gcol = ge * TC + jnp.where(cols < 192, cols, cols - EXT_C)
    inside = (grow >= 0) & (grow < N_NORTH * TR) & (gcol >= 0) & (gcol < N_EAST * TC)

    even_north = (north & 1) == 0
    even_east = (east & 1) == 0
    lane = lax.broadcasted_iota(jnp.int32, (8, 128), 1)
    ext = []
    for k in range(5):
        a, b = across_e_ref[k], beside_e_ref[k]
        w, e = jnp.where(even_east, b, a), jnp.where(even_east, a, b)
        a, b = across_n_ref[k], beside_n_ref[k]
        from_north, from_south = jnp.where(even_north, b, a), jnp.where(even_north, a, b)
        a, b = across_n_ref[5 + k], beside_n_ref[5 + k]
        n, s = jnp.where(even_north, b, a), jnp.where(even_north, a, b)
        corner_w = jnp.where(lane < 64, s, n)
        corner_e = jnp.where(lane < 64, shifted(s, 64, 1), shifted(n, 64, 1))
        sides = jnp.concatenate([e, corner_e, jnp.zeros((96, 128), f32), corner_w, w], axis=0).T

        def ends(rows):
            return jnp.where(lane < 64, shifted(rows, -8, 1), shifted(rows, 8, 1))

        left = jnp.concatenate([fields_ref[k], from_south, from_north], axis=0)
        right = jnp.concatenate([sides, ends(sides[0:8]), ends(sides[120:128])], axis=0)
        full = jnp.concatenate([left, right], axis=1)
        ext.append(jnp.where(inside, full, 0.0))
    v0, diag, along_east, along_south, cross = ext

    def laplace(u, u_l, u_r, u_u, u_d):
        return jnp.where(inside, u_l + u_r + u_u + u_d - 4.0 * u, 0.0)

    def operate(u):
        u_r = shifted(u, -1, 1)
        u_l = shifted(u, 1, 1)
        u_d = shifted(u, -1, 0)
        u_u = shifted(u, 1, 0)
        lu = laplace(u, u_l, u_r, u_u, u_d)
        llu = laplace(lu, shifted(lu, 1, 1), shifted(lu, -1, 1), shifted(lu, 1, 0), shifted(lu, -1, 0))
        u_rd = shifted(u_r, -1, 0)
        out = diag * u + along_east * u_r + along_south * u_d + cross * u_rd
        out = out + shifted(along_east * u + cross * u_d, 1, 1)
        out = out + shifted(along_south * u + cross * u_r + shifted(cross * u, 1, 1), 1, 0)
        return (out + (1.0 - TENSION) * llu - TENSION * lu) * SHRINK

    v = [v0]
    for _ in range(3):
        v.append(operate(v[-1]))
    own = [a[0:TR, 0:TC] for a in v]
    for k in range(4):
        basis_ref[k] = own[k]
    pairs = [(0, 0), (0, 1), (1, 1), (1, 2), (2, 2), (2, 3)]
    lane = lax.broadcasted_iota(jnp.int32, (TILES, 128), 1)
    out = jnp.zeros((TILES, 128), f32)
    for k, (p, q) in enumerate(pairs):
        m = jnp.sum(jnp.sum(own[p] * own[q], axis=0, keepdims=True), axis=1, keepdims=True)
        out = jnp.where(lane == k, m, out)
    moments_ref[...] = out


def finish_kernel(moments_ref, basis_ref, surface_ref, residual_ref):
    total = jnp.sum(moments_ref[...], axis=0, keepdims=True)
    m = [total[:, k:k + 1] for k in range(6)]

    def dot(p, q, shift):
        terms = [p[a] * q[b] * m[a + b + shift] for a in range(len(p)) for b in range(len(q))]
        s = terms[0]
        for t in terms[1:]:
            s = s + t
        return s

    one = jnp.ones_like(m[0])
    res = [one]
    direction = [one]
    surf = []
    rr = m[0]
    for it in range(3):
        alpha = rr / dot(direction, direction, 1)
        surf = [(surf[k] if k < len(surf) else 0.0) + alpha * direction[k] for k in range(len(direction))]
        stepped = [jnp.zeros_like(one)] + [alpha * c for c in direction]
        res = [(res[k] if k < len(res) else 0.0) - stepped[k] for k in range(len(stepped))]
        if it < 2:
            fresh = dot(res, res, 0)
            beta = fresh / rr
            direction = [res[k] + (beta * direction[k] if k < len(direction) else 0.0) for k in range(len(res))]
            rr = fresh
    basis = [basis_ref[k] for k in range(4)]
    out = (surf[0] * SHRINK) * basis[0]
    for k in range(1, 3):
        out = out + (surf[k] * SHRINK) * basis[k]
    surface_ref[...] = out
    out = res[0] * basis[0]
    for k in range(1, 4):
        out = out + res[k] * basis[k]
    residual_ref[...] = out


def swaps(count):
    across = [(i, i ^ 1) for i in range(count)]
    beside = [(0, 0), (count - 1, count - 1)]
    for i in range(1, count - 1, 2):
        beside += [(i, i + 1), (i + 1, i)]
    return across, sorted(beside)


def body(destinations, cells, fractions, weights, heights, counts):
    params = pltpu.CompilerParams(vmem_limit_bytes=40 * 1024 * 1024)
    row = lax.broadcasted_iota(jnp.int32, (16, 128), 0)
    place = jnp.where(row < 8, lax.axis_index("north"), lax.axis_index("east")).astype(jnp.int32)
    block = (BLK_DEV, 128)
    send = pl.pallas_call(
        route_kernel,
        out_shape=pltpu.VMEM((TILES, 5, MOST, 128), f32),
        in_specs=[whole(pltpu.HBM), whole(pltpu.SMEM)] + [whole(pltpu.HBM)] * 4,
        out_specs=whole(),
        scratch_shapes=[
            pltpu.SMEM((BLK_DEV,), jnp.int32),
            pltpu.SMEM((TILES,), jnp.int32),
            pltpu.SMEM((BLK_DEV,), jnp.int32),
            pltpu.VMEM(block, jnp.int32),
            pltpu.VMEM((BLK_DEV, 2, 128), f32),
            pltpu.VMEM(block, f32),
            pltpu.VMEM(block, f32),
            pltpu.VMEM((5, BLK_DEV, 128), f32),
            pltpu.SemaphoreType.DMA((5,)),
        ],
        compiler_params=pltpu.CompilerParams(vmem_limit_bytes=62_050_000),
    )(destinations.reshape(BLK_DEV), counts, cells, fractions, weights, heights)
    got = lax.all_to_all(send, AXES, split_axis=0, concat_axis=0, tiled=True)
    strip = jax.ShapeDtypeStruct((5, 8, 128), f32)
    fields, top, bottom, across, beside = pl.pallas_call(
        gather_kernel,
        out_shape=[jax.ShapeDtypeStruct((5, TR, TC), f32)] + [strip] * 4,
        in_specs=[whole()] * 2,
        out_specs=[whole()] * 5,
        scratch_shapes=[
            pltpu.VMEM((PAIRS, 5, 128, 256), f32),
            pltpu.VMEM((16 * PAIRS, 128), jnp.int32),
            pltpu.SMEM((16 * PAIRS, 128), jnp.int32),
            pltpu.SMEM((3, PAIRS * STEPS * WINDOWS + 8), jnp.int32),
            pltpu.VMEM((8, 2, 28 * UNITS, 128), f32),
            pltpu.VMEM((BANDS * REACH, 128), f32),
            pltpu.SemaphoreType.DMA,
        ],
        compiler_params=params,
    )(place, got)
    east_across, east_beside = swaps(N_EAST)
    north_across, north_beside = swaps(N_NORTH)
    beside_e = lax.ppermute(beside, "east", east_beside)
    across_e = lax.ppermute(across, "east", east_across)
    message = jax.ShapeDtypeStruct((10, 8, 128), f32)
    to_across, to_beside = pl.pallas_call(
        corner_kernel,
        out_shape=[message] * 2,
        in_specs=[whole()] * 5,
        out_specs=[whole()] * 2,
        compiler_params=params,
    )(place, top, bottom, across_e, beside_e)
    beside_n = lax.ppermute(to_beside, "north", north_beside)
    across_n = lax.ppermute(to_across, "north", north_across)
    basis, moments = pl.pallas_call(
        krylov_kernel,
        out_shape=[jax.ShapeDtypeStruct((4, TR, TC), f32), jax.ShapeDtypeStruct((TILES, 128), f32)],
        in_specs=[whole()] * 6,
        out_specs=[whole()] * 2,
        compiler_params=params,
    )(place, fields, across_e, beside_e, across_n, beside_n)
    spread = lax.all_to_all(moments, AXES, split_axis=0, concat_axis=0, tiled=True)
    return pl.pallas_call(
        finish_kernel,
        out_shape=[jax.ShapeDtypeStruct((TR, TC), f32)] * 2,
        in_specs=[whole()] * 2,
        out_specs=[whole()] * 2,
        compiler_params=params,
    )(spread, basis)


def solution(mesh):
    return jax.shard_map(
        body,
        mesh=mesh,
        in_specs=(
            P(AXES, None),
            P(AXES, None),
            P(AXES, None, None),
            P(AXES, None),
            P(AXES, None),
            P(AXES),
        ),
        out_specs=(P("north", "east"), P("north", "east")),
        check_vma=False,
    )
```

```python
import jax
import jax.numpy as jnp
from jax import lax
from jax.experimental import pallas as pl
from jax.experimental.pallas import tpu as pltpu
from jax.sharding import PartitionSpec as P

TR = 128
TC = 128
BLK_DEV = 256
MOST = 4
N_NORTH = 4
N_EAST = 32
TILES = N_NORTH * N_EAST
SHRINK = 1.0 / 64.0
TENSION = 0.75
AXES = ("north", "east")
f32 = jnp.float32
bf16 = jnp.bfloat16

UNITS = 8
GROUPS = TILES * MOST // 128
PAIRS = GROUPS // 2
HALF = 24
WINDOW = 2 * HALF
BANDS = 16
TWO_HOT = 10
SPILL = BANDS * HALF
REACH = 176
STEPS = 128 // UNITS
WINDOWS = -(-127 // WINDOW)


def whole(space=pltpu.VMEM):
    return pl.BlockSpec(memory_space=space)


def row_of(cell):
    return jnp.floor((cell + 0.5) * (1.0 / 127.0))


def sort_lanes(keys):
    lane = lax.broadcasted_iota(jnp.int32, keys.shape, 1)
    size = 2
    while size <= 128:
        gap = size // 2
        while gap >= 1:
            low = (lane & gap) == 0
            other = jnp.take_along_axis(keys, lane ^ gap, axis=1)
            take_min = low == ((lane & size) == 0)
            keys = jnp.where(take_min, jnp.minimum(keys, other), jnp.maximum(keys, other))
            gap //= 2
        size *= 2
    return keys


def route_kernel(dest_hbm, count_ref, cells_hbm, frac_hbm, weight_hbm, height_hbm, out_ref,
                 dest_ref, seen_ref, slot_ref, cells_ref, frac_ref, weight_ref, height_ref, sorted_ref, sems):
    copies = [
        pltpu.make_async_copy(src, dst, sems.at[k])
        for k, (src, dst) in enumerate([
            (dest_hbm, dest_ref), (cells_hbm, cells_ref), (frac_hbm, frac_ref),
            (weight_hbm, weight_ref), (height_hbm, height_ref)])
    ]
    for c in copies:
        c.start()

    def clear(k, _):
        seen_ref[k] = 0
        out_ref[k, 3] = jnp.zeros((MOST, 128), f32)
        return 0

    lax.fori_loop(0, TILES, clear, 0, unroll=8)
    for c in copies[:2]:
        c.wait()
    for b in range(BLK_DEV):
        tile = dest_ref[b]
        rank = seen_ref[tile]
        seen_ref[tile] = rank + 1
        slot_ref[b] = rank
    cell = cells_ref[...].astype(f32)
    lane = lax.broadcasted_iota(jnp.int32, cell.shape, 1).astype(f32)
    keys = sort_lanes(row_of(cell) * 128.0 + lane)
    source = (keys - 128.0 * jnp.floor(keys * (1.0 / 128.0))).astype(jnp.int32)
    for c in copies[2:]:
        c.wait()
    live = lax.broadcasted_iota(jnp.int32, cell.shape, 0) < count_ref[0]
    weight = jnp.where(live, weight_ref[...], 0.0)
    values = [cell, frac_ref[:, 0, :], frac_ref[:, 1, :], weight, height_ref[...]]
    for f, v in enumerate(values):
        sorted_ref[f] = jnp.take_along_axis(v, source, axis=1)

    for b in range(BLK_DEV):
        tile = dest_ref[b]
        rank = slot_ref[b]
        for f in range(5):
            out_ref[tile, f, pl.ds(rank, 1), :] = sorted_ref[f, b:b + 1, :]


def high_low(value):
    high = value.astype(bf16).astype(f32)
    return [high, value - high]


def build(rank, base, pair, group, by_rank_ref, vals_ref):
    lanes_in = slice(group * 128, group * 128 + 128)
    cell, d, e, mass, height = [by_rank_ref[pair, f, pl.ds(rank, UNITS), lanes_in] for f in range(5)]
    i = row_of(cell)
    j = cell - 127.0 * i
    inner = i - base.astype(f32)
    lower = inner >= float(HALF)
    i_in = jnp.where((inner >= 0.0) & (inner < float(WINDOW)), jnp.where(lower, inner - float(HALF), inner), -100.0)
    place = j + jnp.where(lower, 128.0, 0.0)
    a0, a1, b0, b1 = 1.0 - d, d, 1.0 - e, e
    mh = mass * height
    cols = [mass * b0 * b0, mass * b1 * b1, mass * b0 * b1]
    ends = [mh * b0, mh * b1]
    down, up, mid = [], [], []
    for c in cols:
        down += high_low(c * a1 * a1)
        up += high_low(c * a0 * a0)
        mid += high_low(c * a0 * a1)
    for c in ends:
        down += high_low(c * a1)
        up += high_low(c * a0)
    for k, v in enumerate(down + up + mid + [i_in, place]):
        vals_ref[group, k * UNITS:(k + 1) * UNITS, :] = v
    iota = lax.broadcasted_iota(jnp.int32, (16, 128), 0).astype(f32).astype(bf16)
    zero = jnp.zeros((16, 128), bf16)
    one = jnp.ones((16, 128), bf16)

    def row(k, s):
        return jnp.broadcast_to(vals_ref[group, k * UNITS + s:k * UNITS + s + 1, :], (16, 128))

    eighth = jnp.where(iota < 8.0, iota, iota - 8.0) + 16.0
    first = iota < 8.0
    lefts, rights = [], []
    for s in range(UNITS):
        i_row = row(26, s)
        i_b = i_row.astype(bf16)
        i_next = (i_row + 1.0).astype(bf16)
        at, at_end = iota == i_b, eighth == i_b
        after, after_end = iota == i_next, eighth == i_next
        pieces = []
        for k in range(0, TWO_HOT, 2):
            v1 = [row(k + n, s).astype(bf16) for n in range(2)]
            v0 = [row(TWO_HOT + k + n, s).astype(bf16) for n in range(2)]
            for n in range(2):
                pieces.append(jnp.where(at, v0[n], jnp.where(after, v1[n], zero)))
            pieces.append(jnp.where(at_end, jnp.where(first, v0[0], v0[1]),
                                    jnp.where(after_end, jnp.where(first, v1[0], v1[1]), zero)))
        for k in range(2 * TWO_HOT, 2 * TWO_HOT + BANDS - TWO_HOT, 2):
            v = [row(k + n, s).astype(bf16) for n in range(2)]
            for n in range(2):
                pieces.append(jnp.where(at, v[n], zero))
            pieces.append(jnp.where(at_end, jnp.where(first, v[0], v[1]), zero))
        spill = vals_ref[group, pl.ds(s, 16, stride=UNITS), :]
        pieces.append(jnp.where(i_row == float(HALF - 1), spill, 0.0).astype(bf16))
        lefts.append(jnp.concatenate(pieces, axis=0))
        p_b = row(27, s).astype(bf16)
        rights.append(jnp.concatenate([jnp.where((iota + float(16 * g)) == p_b, one, zero) for g in range(16)], axis=0))
    return lefts, rights


def shifted(a, by, axis):
    return pltpu.roll(a, by % a.shape[axis], axis)


def gather_kernel(place_ref, x_ref, fields_ref, top_ref, bottom_ref, across_ref, beside_ref,
                  by_rank_ref, bounds_ref, limits_ref, items_ref, vals_ref, acc_ref, sem):
    def by_rank(p, g, f):
        first = (2 * p + g) * 32
        return x_ref[first:first + 32, f].reshape(128, 128).T

    def keep(p, g, f, value):
        by_rank_ref[p, f, :, g * 128:g * 128 + 128] = value

    for p in range(PAIRS):
        least, most = [], []
        for g in range(2):
            mass = by_rank(p, g, 3)
            live = mass > 0.0
            cell = jnp.where(live, by_rank(p, g, 0), 0.0)
            keep(p, g, 3, jnp.where(live, mass, 0.0))
            keep(p, g, 0, cell)
            i = row_of(cell)
            least.append(jnp.where(live, i, 1000.0))
            most.append(jnp.where(live, i, -1.0))
        low = jnp.min(jnp.minimum(least[0], least[1]).T, axis=0, keepdims=True)
        high = jnp.max(jnp.maximum(most[0], most[1]).T, axis=0, keepdims=True)
        base = jnp.floor(low * 0.125) * 8.0
        span = shifted(high, -(UNITS - 1), 1) - base
        starts = (lax.broadcasted_iota(jnp.int32, (1, 128), 1) & (UNITS - 1)) == 0
        widest = jnp.max(jnp.where(starts, span, -1.0), axis=1, keepdims=True)
        for n, v in enumerate([base, span, jnp.broadcast_to(widest, (1, 128))]):
            at = 8 * (3 * p + n)
            bounds_ref[at:at + 8, :] = jnp.broadcast_to(v, (8, 128)).astype(jnp.int32)
    copy = pltpu.make_async_copy(bounds_ref, limits_ref, sem)
    copy.start()
    acc_ref[...] = jnp.zeros_like(acc_ref)
    for p in range(PAIRS):
        for g in range(2):
            live = by_rank_ref[p, 3, :, g * 128:g * 128 + 128] > 0.0
            for f in (1, 2, 4):
                keep(p, g, f, jnp.where(live, by_rank(p, g, f), 0.0))
    copy.wait()

    sub = lax.broadcasted_iota(jnp.int32, (8, 128), 0)

    def item(rank, pair, base, half):
        rank = pl.multiple_of(rank, UNITS)
        lefts, rights = [], []
        for g in range(2):
            more = build(rank, base, pair, g, by_rank_ref, vals_ref.at[half])
            lefts += more[0]
            rights += more[1]
        out = lax.dot_general(
            jnp.concatenate(lefts, axis=1), jnp.concatenate(rights, axis=1),
            (((1,), (1,)), ((), ())), preferred_element_type=f32)
        base = pl.multiple_of(jnp.where(base > 127, 0, base), 8)
        for k in range(0, BANDS, 2):
            for n in range(2):
                for h in range(2):
                    start = (k + n) * REACH + base + h * HALF
                    cols = slice(h * 128, h * 128 + 128)
                    line = k * HALF + 16 * n
                    acc_ref[pl.ds(start, 16), :] += out[line:line + 16, cols]
                    line = k * HALF + 32 + 8 * n
                    acc_ref[pl.ds(start + 16, 8), :] += out[line:line + 8, cols]
        for k in range(TWO_HOT):
            for h in range(2):
                rows = pl.ds(k * REACH + base + (h + 1) * HALF, 8)
                acc_ref[rows, :] += jnp.where(sub == 0, out[SPILL + k:SPILL + k + 1, h * 128:(h + 1) * 128], 0.0)

    def eight(c, _):
        for n in range(8):
            rank = (4 * c + n // 2) * UNITS
            item(rank, n % 2, limits_ref[24 * (n % 2), rank], n)
        return 0

    lax.fori_loop(0, PAIRS * STEPS // 8, eight, 0)

    @pl.when((limits_ref[16, 0] >= WINDOW) | (limits_ref[40, 0] >= WINDOW))
    def _():
        def listed(q, count):
            for p in range(PAIRS):
                base = limits_ref[24 * p, q * UNITS]
                span = limits_ref[24 * p + 8, q * UNITS]
                for w in range(1, WINDOWS):
                    items_ref[0, count] = q * UNITS
                    items_ref[1, count] = base + w * WINDOW
                    items_ref[2, count] = p
                    count = count + (span >= w * WINDOW).astype(jnp.int32)
            return count

        count = lax.fori_loop(0, STEPS, listed, jnp.int32(0))
        items_ref[0, count] = 0
        items_ref[1, count] = 1000
        items_ref[2, count] = 0

        def two(c, _):
            for n in range(2):
                t = 2 * c + n
                item(items_ref[0, t], items_ref[2, t], items_ref[1, t], n)
            return 0

        lax.fori_loop(0, (count + 1) // 2, two, 0)

    def band(k):
        return acc_ref[k * REACH:k * REACH + TR, :]

    def pair(k):
        return band(k) + band(k + 1)

    diag = pair(0) + shifted(pair(2), 1, 1)
    along_east = pair(4)
    rhs = pair(6) + shifted(pair(8), 1, 1)
    along_south = pair(10) + shifted(pair(12), 1, 1)
    cross = pair(14)
    even = (place_ref[8:16, :] & 1) == 0
    for k, v in enumerate([rhs, diag, along_east, along_south, cross]):
        fields_ref[k] = v
        top_ref[k] = v[0:8]
        bottom_ref[k] = v[120:128]
        t = v.T
        west, east = t[0:8], t[120:128]
        across_ref[k] = jnp.where(even, east, west)
        beside_ref[k] = jnp.where(even, west, east)


def corner_kernel(place_ref, top_ref, bottom_ref, across_ref, beside_ref, to_across_ref, to_beside_ref):
    lane = lax.broadcasted_iota(jnp.int32, (8, 128), 1)
    even_north = (place_ref[0:8, :] & 1) == 0
    even_east = (place_ref[8:16, :] & 1) == 0
    for k in range(5):
        a, b = across_ref[k], beside_ref[k]
        w = jnp.where(even_east, b, a)
        e = shifted(jnp.where(even_east, a, b), 64, 1)
        north = jnp.where(lane < 64, w, e)
        south = jnp.where(lane >= 64, w, e)
        top, bottom = top_ref[k], bottom_ref[k]
        to_across_ref[k] = jnp.where(even_north, bottom, top)
        to_beside_ref[k] = jnp.where(even_north, top, bottom)
        to_across_ref[5 + k] = jnp.where(even_north, south, north)
        to_beside_ref[5 + k] = jnp.where(even_north, north, south)


EXT_R = 144
EXT_C = 256


def krylov_kernel(place_ref, fields_ref, across_e_ref, beside_e_ref, across_n_ref, beside_n_ref,
                  basis_ref, moments_ref):
    north, east = place_ref[0:8, :], place_ref[8:16, :]
    gn = jnp.concatenate([jnp.concatenate([north] * (EXT_R // 8), axis=0)] * 2, axis=1)
    ge = jnp.concatenate([jnp.concatenate([east] * (EXT_R // 8), axis=0)] * 2, axis=1)
    rows = lax.broadcasted_iota(jnp.int32, (EXT_R, EXT_C), 0)
    cols = lax.broadcasted_iota(jnp.int32, (EXT_R, EXT_C), 1)
    grow = gn * TR + jnp.where(rows < 136, rows, rows - EXT_R)
    gcol = ge * TC + jnp.where(cols < 192, cols, cols - EXT_C)
    inside = (grow >= 0) & (grow < N_NORTH * TR) & (gcol >= 0) & (gcol < N_EAST * TC)

    even_north = (north & 1) == 0
    even_east = (east & 1) == 0
    lane = lax.broadcasted_iota(jnp.int32, (8, 128), 1)
    ext = []
    for k in range(5):
        a, b = across_e_ref[k], beside_e_ref[k]
        w, e = jnp.where(even_east, b, a), jnp.where(even_east, a, b)
        a, b = across_n_ref[k], beside_n_ref[k]
        from_north, from_south = jnp.where(even_north, b, a), jnp.where(even_north, a, b)
        a, b = across_n_ref[5 + k], beside_n_ref[5 + k]
        n, s = jnp.where(even_north, b, a), jnp.where(even_north, a, b)
        corner_w = jnp.where(lane < 64, s, n)
        corner_e = jnp.where(lane < 64, shifted(s, 64, 1), shifted(n, 64, 1))
        sides = jnp.concatenate([e, corner_e, jnp.zeros((96, 128), f32), corner_w, w], axis=0).T

        def ends(rows):
            return jnp.where(lane < 64, shifted(rows, -8, 1), shifted(rows, 8, 1))

        left = jnp.concatenate([fields_ref[k], from_south, from_north], axis=0)
        right = jnp.concatenate([sides, ends(sides[0:8]), ends(sides[120:128])], axis=0)
        full = jnp.concatenate([left, right], axis=1)
        ext.append(jnp.where(inside, full, 0.0))
    v0, diag, along_east, along_south, cross = ext

    def laplace(u, u_l, u_r, u_u, u_d):
        return jnp.where(inside, u_l + u_r + u_u + u_d - 4.0 * u, 0.0)

    def operate(u):
        u_r = shifted(u, -1, 1)
        u_l = shifted(u, 1, 1)
        u_d = shifted(u, -1, 0)
        u_u = shifted(u, 1, 0)
        lu = laplace(u, u_l, u_r, u_u, u_d)
        llu = laplace(lu, shifted(lu, 1, 1), shifted(lu, -1, 1), shifted(lu, 1, 0), shifted(lu, -1, 0))
        u_rd = shifted(u_r, -1, 0)
        out = diag * u + along_east * u_r + along_south * u_d + cross * u_rd
        out = out + shifted(along_east * u + cross * u_d, 1, 1)
        out = out + shifted(along_south * u + cross * u_r + shifted(cross * u, 1, 1), 1, 0)
        return (out + (1.0 - TENSION) * llu - TENSION * lu) * SHRINK

    v = [v0]
    for _ in range(3):
        v.append(operate(v[-1]))
    own = [a[0:TR, 0:TC] for a in v]
    for k in range(4):
        basis_ref[k] = own[k]
    pairs = [(0, 0), (0, 1), (1, 1), (1, 2), (2, 2), (2, 3)]
    lane = lax.broadcasted_iota(jnp.int32, (TILES, 8), 1)
    out = jnp.zeros((TILES, 8), f32)
    for k, (p, q) in enumerate(pairs):
        m = jnp.sum(jnp.sum(own[p] * own[q], axis=0, keepdims=True), axis=1, keepdims=True)
        out = jnp.where(lane == k, m, out)
    moments_ref[...] = out


def finish_kernel(moments_ref, basis_ref, surface_ref, residual_ref):
    total = jnp.sum(moments_ref[...], axis=0, keepdims=True)
    m = [total[:, k:k + 1] for k in range(6)]

    def dot(p, q, shift):
        terms = [p[a] * q[b] * m[a + b + shift] for a in range(len(p)) for b in range(len(q))]
        s = terms[0]
        for t in terms[1:]:
            s = s + t
        return s

    one = jnp.ones_like(m[0])
    res = [one]
    direction = [one]
    surf = []
    rr = m[0]
    for it in range(3):
        alpha = rr / dot(direction, direction, 1)
        surf = [(surf[k] if k < len(surf) else 0.0) + alpha * direction[k] for k in range(len(direction))]
        stepped = [jnp.zeros_like(one)] + [alpha * c for c in direction]
        res = [(res[k] if k < len(res) else 0.0) - stepped[k] for k in range(len(stepped))]
        if it < 2:
            fresh = dot(res, res, 0)
            beta = fresh / rr
            direction = [res[k] + (beta * direction[k] if k < len(direction) else 0.0) for k in range(len(res))]
            rr = fresh
    basis = [basis_ref[k] for k in range(4)]
    out = (surf[0] * SHRINK) * basis[0]
    for k in range(1, 3):
        out = out + (surf[k] * SHRINK) * basis[k]
    surface_ref[...] = out
    out = res[0] * basis[0]
    for k in range(1, 4):
        out = out + res[k] * basis[k]
    residual_ref[...] = out


def swaps(count):
    across = [(i, i ^ 1) for i in range(count)]
    beside = [(0, 0), (count - 1, count - 1)]
    for i in range(1, count - 1, 2):
        beside += [(i, i + 1), (i + 1, i)]
    return across, sorted(beside)


def body(destinations, cells, fractions, weights, heights, counts):
    params = pltpu.CompilerParams(vmem_limit_bytes=40 * 1024 * 1024)
    row = lax.broadcasted_iota(jnp.int32, (16, 128), 0)
    place = jnp.where(row < 8, lax.axis_index("north"), lax.axis_index("east")).astype(jnp.int32)
    block = (BLK_DEV, 128)
    send = pl.pallas_call(
        route_kernel,
        out_shape=pltpu.VMEM((TILES, 5, MOST, 128), f32),
        in_specs=[whole(pltpu.HBM), whole(pltpu.SMEM)] + [whole(pltpu.HBM)] * 4,
        out_specs=whole(),
        scratch_shapes=[
            pltpu.SMEM((BLK_DEV,), jnp.int32),
            pltpu.SMEM((TILES,), jnp.int32),
            pltpu.SMEM((BLK_DEV,), jnp.int32),
            pltpu.VMEM(block, jnp.int32),
            pltpu.VMEM((BLK_DEV, 2, 128), f32),
            pltpu.VMEM(block, f32),
            pltpu.VMEM(block, f32),
            pltpu.VMEM((5, BLK_DEV, 128), f32),
            pltpu.SemaphoreType.DMA((5,)),
        ],
        compiler_params=pltpu.CompilerParams(vmem_limit_bytes=62_050_000),
    )(destinations.reshape(BLK_DEV), counts, cells, fractions, weights, heights)
    got = lax.all_to_all(send, AXES, split_axis=0, concat_axis=0, tiled=True)
    strip = jax.ShapeDtypeStruct((5, 8, 128), f32)
    fields, top, bottom, across, beside = pl.pallas_call(
        gather_kernel,
        out_shape=[jax.ShapeDtypeStruct((5, TR, TC), f32)] + [strip] * 4,
        in_specs=[whole()] * 2,
        out_specs=[whole()] * 5,
        scratch_shapes=[
            pltpu.VMEM((PAIRS, 5, 128, 256), f32),
            pltpu.VMEM((24 * PAIRS, 128), jnp.int32),
            pltpu.SMEM((24 * PAIRS, 128), jnp.int32),
            pltpu.SMEM((3, PAIRS * STEPS * WINDOWS + 8), jnp.int32),
            pltpu.VMEM((8, 2, 28 * UNITS, 128), f32),
            pltpu.VMEM((BANDS * REACH, 128), f32),
            pltpu.SemaphoreType.DMA,
        ],
        compiler_params=params,
    )(place, got)
    east_across, east_beside = swaps(N_EAST)
    north_across, north_beside = swaps(N_NORTH)
    beside_e = lax.ppermute(beside, "east", east_beside)
    across_e = lax.ppermute(across, "east", east_across)
    message = jax.ShapeDtypeStruct((10, 8, 128), f32)
    to_across, to_beside = pl.pallas_call(
        corner_kernel,
        out_shape=[message] * 2,
        in_specs=[whole()] * 5,
        out_specs=[whole()] * 2,
        compiler_params=params,
    )(place, top, bottom, across_e, beside_e)
    beside_n = lax.ppermute(to_beside, "north", north_beside)
    across_n = lax.ppermute(to_across, "north", north_across)
    basis, moments = pl.pallas_call(
        krylov_kernel,
        out_shape=[jax.ShapeDtypeStruct((4, TR, TC), f32), jax.ShapeDtypeStruct((TILES, 8), f32)],
        in_specs=[whole()] * 6,
        out_specs=[whole()] * 2,
        compiler_params=params,
    )(place, fields, across_e, beside_e, across_n, beside_n)
    spread = lax.all_to_all(moments, AXES, split_axis=0, concat_axis=0, tiled=True)
    return pl.pallas_call(
        finish_kernel,
        out_shape=[jax.ShapeDtypeStruct((TR, TC), f32)] * 2,
        in_specs=[whole()] * 2,
        out_specs=[whole()] * 2,
        compiler_params=params,
    )(spread, basis)


def solution(mesh):
    return jax.shard_map(
        body,
        mesh=mesh,
        in_specs=(
            P(AXES, None),
            P(AXES, None),
            P(AXES, None, None),
            P(AXES, None),
            P(AXES, None),
            P(AXES),
        ),
        out_specs=(P("north", "east"), P("north", "east")),
        check_vma=False,
    )
```

```python
import jax
import jax.numpy as jnp
from jax import lax
from jax.experimental import pallas as pl
from jax.experimental.pallas import tpu as pltpu
from jax.sharding import PartitionSpec as P

TR = 128
TC = 128
BLK_DEV = 256
MOST = 4
N_NORTH = 4
N_EAST = 32
TILES = N_NORTH * N_EAST
SHRINK = 1.0 / 64.0
TENSION = 0.75
AXES = ("north", "east")
f32 = jnp.float32
bf16 = jnp.bfloat16

UNITS = 8
GROUPS = TILES * MOST // 128
PAIRS = GROUPS // 2
HALF = 24
WINDOW = 2 * HALF
BANDS = 16
TWO_HOT = 10
SPILL = BANDS * HALF
REACH = 176
STEPS = 128 // UNITS
WINDOWS = -(-127 // WINDOW)


def whole(space=pltpu.VMEM):
    return pl.BlockSpec(memory_space=space)


def row_of(cell):
    return jnp.floor((cell + 0.5) * (1.0 / 127.0))


def sort_lanes(keys):
    lane = lax.broadcasted_iota(jnp.int32, keys.shape, 1)
    size = 2
    while size <= 128:
        gap = size // 2
        while gap >= 1:
            low = (lane & gap) == 0
            other = jnp.take_along_axis(keys, lane ^ gap, axis=1)
            take_min = low == ((lane & size) == 0)
            keys = jnp.where(take_min, jnp.minimum(keys, other), jnp.maximum(keys, other))
            gap //= 2
        size *= 2
    return keys


def route_kernel(dest_hbm, count_ref, cells_hbm, frac_hbm, weight_hbm, height_hbm, out_ref,
                 dest_ref, seen_ref, slot_ref, cells_ref, frac_ref, weight_ref, height_ref, sorted_ref, sems):
    copies = [
        pltpu.make_async_copy(src, dst, sems.at[k])
        for k, (src, dst) in enumerate([
            (dest_hbm, dest_ref), (cells_hbm, cells_ref), (frac_hbm, frac_ref),
            (weight_hbm, weight_ref), (height_hbm, height_ref)])
    ]
    for c in copies:
        c.start()

    def clear(k, _):
        seen_ref[k] = 0
        out_ref[k, 3] = jnp.zeros((MOST, 128), f32)
        return 0

    lax.fori_loop(0, TILES, clear, 0, unroll=8)
    for c in copies[:2]:
        c.wait()
    for b in range(BLK_DEV):
        tile = dest_ref[b]
        rank = seen_ref[tile]
        seen_ref[tile] = rank + 1
        slot_ref[b] = rank
    cell = cells_ref[...].astype(f32)
    lane = lax.broadcasted_iota(jnp.int32, cell.shape, 1).astype(f32)
    keys = sort_lanes(row_of(cell) * 128.0 + lane)
    source = (keys - 128.0 * jnp.floor(keys * (1.0 / 128.0))).astype(jnp.int32)
    for c in copies[2:]:
        c.wait()
    live = lax.broadcasted_iota(jnp.int32, cell.shape, 0) < count_ref[0]
    weight = jnp.where(live, weight_ref[...], 0.0)
    values = [cell, frac_ref[:, 0, :], frac_ref[:, 1, :], weight, height_ref[...]]
    for f, v in enumerate(values):
        sorted_ref[f] = jnp.take_along_axis(v, source, axis=1)

    for b in range(BLK_DEV):
        tile = dest_ref[b]
        rank = slot_ref[b]
        for f in range(5):
            out_ref[tile, f, pl.ds(rank, 1), :] = sorted_ref[f, b:b + 1, :]


def high_low(value):
    high = value.astype(bf16).astype(f32)
    return [high, value - high]


def build(rank, base, pair, group, by_rank_ref, vals_ref):
    lanes_in = slice(group * 128, group * 128 + 128)
    cell, d, e, mass, height = [by_rank_ref[pair, f, pl.ds(rank, UNITS), lanes_in] for f in range(5)]
    i = row_of(cell)
    j = cell - 127.0 * i
    inner = i - base.astype(f32)
    lower = inner >= float(HALF)
    i_in = jnp.where((inner >= 0.0) & (inner < float(WINDOW)), jnp.where(lower, inner - float(HALF), inner), -100.0)
    place = j + jnp.where(lower, 128.0, 0.0)
    a0, a1, b0, b1 = 1.0 - d, d, 1.0 - e, e
    mh = mass * height
    cols = [mass * b0 * b0, mass * b1 * b1, mass * b0 * b1]
    ends = [mh * b0, mh * b1]
    down, up, mid = [], [], []
    for c in cols:
        down += high_low(c * a1 * a1)
        up += high_low(c * a0 * a0)
        mid += high_low(c * a0 * a1)
    for c in ends:
        down += high_low(c * a1)
        up += high_low(c * a0)
    for k, v in enumerate(down + up + mid + [i_in, place]):
        vals_ref[group, k * UNITS:(k + 1) * UNITS, :] = v
    iota = lax.broadcasted_iota(jnp.int32, (16, 128), 0).astype(f32).astype(bf16)
    zero = jnp.zeros((16, 128), bf16)
    one = jnp.ones((16, 128), bf16)

    def row(k, s):
        return jnp.broadcast_to(vals_ref[group, k * UNITS + s:k * UNITS + s + 1, :], (16, 128))

    eighth = jnp.where(iota < 8.0, iota, iota - 8.0) + 16.0
    first = iota < 8.0
    lefts, rights = [], []
    for s in range(UNITS):
        i_row = row(26, s)
        i_b = i_row.astype(bf16)
        i_next = (i_row + 1.0).astype(bf16)
        at, at_end = iota == i_b, eighth == i_b
        after, after_end = iota == i_next, eighth == i_next
        pieces = []
        for k in range(0, TWO_HOT, 2):
            v1 = [row(k + n, s).astype(bf16) for n in range(2)]
            v0 = [row(TWO_HOT + k + n, s).astype(bf16) for n in range(2)]
            for n in range(2):
                pieces.append(jnp.where(at, v0[n], jnp.where(after, v1[n], zero)))
            pieces.append(jnp.where(at_end, jnp.where(first, v0[0], v0[1]),
                                    jnp.where(after_end, jnp.where(first, v1[0], v1[1]), zero)))
        for k in range(2 * TWO_HOT, 2 * TWO_HOT + BANDS - TWO_HOT, 2):
            v = [row(k + n, s).astype(bf16) for n in range(2)]
            for n in range(2):
                pieces.append(jnp.where(at, v[n], zero))
            pieces.append(jnp.where(at_end, jnp.where(first, v[0], v[1]), zero))
        spill = vals_ref[group, pl.ds(s, 16, stride=UNITS), :]
        pieces.append(jnp.where(i_row == float(HALF - 1), spill, 0.0).astype(bf16))
        lefts.append(jnp.concatenate(pieces, axis=0))
        p_b = row(27, s).astype(bf16)
        rights.append(jnp.concatenate([jnp.where((iota + float(16 * g)) == p_b, one, zero) for g in range(16)], axis=0))
    return lefts, rights


def shifted(a, by, axis):
    return pltpu.roll(a, by % a.shape[axis], axis)


def gather_kernel(place_ref, x_ref, fields_ref, top_ref, bottom_ref, across_ref, beside_ref,
                  by_rank_ref, bounds_ref, limits_ref, items_ref, vals_ref, acc_ref, sem):
    def by_rank(p, g, f):
        first = (2 * p + g) * 32
        return x_ref[first:first + 32, f].reshape(128, 128).T

    def keep(p, g, f, value):
        by_rank_ref[p, f, :, g * 128:g * 128 + 128] = value

    for p in range(PAIRS):
        least, most = [], []
        for g in range(2):
            mass = by_rank(p, g, 3)
            live = mass > 0.0
            cell = jnp.where(live, by_rank(p, g, 0), 0.0)
            keep(p, g, 3, jnp.where(live, mass, 0.0))
            keep(p, g, 0, cell)
            i = row_of(cell)
            least.append(jnp.where(live, i, 1000.0))
            most.append(jnp.where(live, i, -1.0))
        low = jnp.min(jnp.minimum(least[0], least[1]).T, axis=0, keepdims=True)
        high = jnp.max(jnp.maximum(most[0], most[1]).T, axis=0, keepdims=True)
        base = jnp.floor(low * 0.125) * 8.0
        span = shifted(high, -(UNITS - 1), 1) - base
        starts = (lax.broadcasted_iota(jnp.int32, (1, 128), 1) & (UNITS - 1)) == 0
        widest = jnp.max(jnp.where(starts, span, -1.0), axis=1, keepdims=True)
        for n, v in enumerate([base, span, jnp.broadcast_to(widest, (1, 128))]):
            at = 8 * (3 * p + n)
            bounds_ref[at:at + 8, :] = jnp.broadcast_to(v, (8, 128)).astype(jnp.int32)
    copy = pltpu.make_async_copy(bounds_ref, limits_ref, sem)
    copy.start()
    acc_ref[...] = jnp.zeros_like(acc_ref)
    for p in range(PAIRS):
        for g in range(2):
            live = by_rank_ref[p, 3, :, g * 128:g * 128 + 128] > 0.0
            for f in (1, 2, 4):
                keep(p, g, f, jnp.where(live, by_rank(p, g, f), 0.0))
    copy.wait()

    sub = lax.broadcasted_iota(jnp.int32, (8, 128), 0)

    def item(rank, pair, base, half):
        rank = pl.multiple_of(rank, UNITS)
        lefts, rights = [], []
        for g in range(2):
            more = build(rank, base, pair, g, by_rank_ref, vals_ref.at[half])
            lefts += more[0]
            rights += more[1]
        out = lax.dot_general(
            jnp.concatenate(lefts, axis=1), jnp.concatenate(rights, axis=1),
            (((1,), (1,)), ((), ())), preferred_element_type=f32)
        base = pl.multiple_of(jnp.where(base > 127, 0, base), 8)
        for k in range(0, BANDS, 2):
            for n in range(2):
                for h in range(2):
                    start = (k + n) * REACH + base + h * HALF
                    cols = slice(h * 128, h * 128 + 128)
                    line = k * HALF + 16 * n
                    acc_ref[pl.ds(start, 16), :] += out[line:line + 16, cols]
                    line = k * HALF + 32 + 8 * n
                    acc_ref[pl.ds(start + 16, 8), :] += out[line:line + 8, cols]
        for k in range(TWO_HOT):
            for h in range(2):
                rows = pl.ds(k * REACH + base + (h + 1) * HALF, 8)
                acc_ref[rows, :] += jnp.where(sub == 0, out[SPILL + k:SPILL + k + 1, h * 128:(h + 1) * 128], 0.0)

    def eight(c, _):
        for n in range(8):
            rank = (4 * c + n // 2) * UNITS
            item(rank, n % 2, limits_ref[24 * (n % 2), rank], n)
        return 0

    lax.fori_loop(0, PAIRS * STEPS // 8, eight, 0)

    @pl.when((limits_ref[16, 0] >= WINDOW) | (limits_ref[40, 0] >= WINDOW))
    def _():
        def listed(q, count):
            for p in range(PAIRS):
                base = limits_ref[24 * p, q * UNITS]
                span = limits_ref[24 * p + 8, q * UNITS]
                for w in range(1, WINDOWS):
                    items_ref[0, count] = q * UNITS
                    items_ref[1, count] = base + w * WINDOW
                    items_ref[2, count] = p
                    count = count + (span >= w * WINDOW).astype(jnp.int32)
            return count

        count = lax.fori_loop(0, STEPS, listed, jnp.int32(0))
        items_ref[0, count] = 0
        items_ref[1, count] = 1000
        items_ref[2, count] = 0

        def two(c, _):
            for n in range(2):
                t = 2 * c + n
                item(items_ref[0, t], items_ref[2, t], items_ref[1, t], n)
            return 0

        lax.fori_loop(0, (count + 1) // 2, two, 0)

    def band(k):
        return acc_ref[k * REACH:k * REACH + TR, :]

    def pair(k):
        return band(k) + band(k + 1)

    diag = pair(0) + shifted(pair(2), 1, 1)
    along_east = pair(4)
    rhs = pair(6) + shifted(pair(8), 1, 1)
    along_south = pair(10) + shifted(pair(12), 1, 1)
    cross = pair(14)
    even = (place_ref[8:16, :] & 1) == 0
    for k, v in enumerate([rhs, diag, along_east, along_south, cross]):
        fields_ref[k] = v
        top_ref[k] = v[0:8]
        bottom_ref[k] = v[120:128]
        t = v.T
        west, east = t[0:8], t[120:128]
        across_ref[k] = jnp.where(even, east, west)
        beside_ref[k] = jnp.where(even, west, east)


def corner_kernel(place_ref, top_ref, bottom_ref, across_ref, beside_ref, to_across_ref, to_beside_ref):
    lane = lax.broadcasted_iota(jnp.int32, (8, 128), 1)
    even_north = (place_ref[0:8, :] & 1) == 0
    even_east = (place_ref[8:16, :] & 1) == 0
    for k in range(5):
        a, b = across_ref[k], beside_ref[k]
        w = jnp.where(even_east, b, a)
        e = shifted(jnp.where(even_east, a, b), 64, 1)
        north = jnp.where(lane < 64, w, e)
        south = jnp.where(lane >= 64, w, e)
        top, bottom = top_ref[k], bottom_ref[k]
        to_across_ref[k] = jnp.where(even_north, bottom, top)
        to_beside_ref[k] = jnp.where(even_north, top, bottom)
        to_across_ref[5 + k] = jnp.where(even_north, south, north)
        to_beside_ref[5 + k] = jnp.where(even_north, north, south)


EXT_R = 144
EXT_C = 256


def krylov_kernel(place_ref, fields_ref, across_e_ref, beside_e_ref, across_n_ref, beside_n_ref,
                  basis_ref, moments_ref):
    north, east = place_ref[0:8, :], place_ref[8:16, :]
    gn = jnp.concatenate([jnp.concatenate([north] * (EXT_R // 8), axis=0)] * 2, axis=1)
    ge = jnp.concatenate([jnp.concatenate([east] * (EXT_R // 8), axis=0)] * 2, axis=1)
    rows = lax.broadcasted_iota(jnp.int32, (EXT_R, EXT_C), 0)
    cols = lax.broadcasted_iota(jnp.int32, (EXT_R, EXT_C), 1)
    grow = gn * TR + jnp.where(rows < 136, rows, rows - EXT_R)
    gcol = ge * TC + jnp.where(cols < 192, cols, cols - EXT_C)
    inside = (grow >= 0) & (grow < N_NORTH * TR) & (gcol >= 0) & (gcol < N_EAST * TC)

    even_north = (north & 1) == 0
    even_east = (east & 1) == 0
    lane = lax.broadcasted_iota(jnp.int32, (8, 128), 1)
    ext = []
    for k in range(5):
        a, b = across_e_ref[k], beside_e_ref[k]
        w, e = jnp.where(even_east, b, a), jnp.where(even_east, a, b)
        a, b = across_n_ref[k], beside_n_ref[k]
        from_north, from_south = jnp.where(even_north, b, a), jnp.where(even_north, a, b)
        a, b = across_n_ref[5 + k], beside_n_ref[5 + k]
        n, s = jnp.where(even_north, b, a), jnp.where(even_north, a, b)
        corner_w = jnp.where(lane < 64, s, n)
        corner_e = jnp.where(lane < 64, shifted(s, 64, 1), shifted(n, 64, 1))
        sides = jnp.concatenate([e, corner_e, jnp.zeros((96, 128), f32), corner_w, w], axis=0).T

        def ends(rows):
            return jnp.where(lane < 64, shifted(rows, -8, 1), shifted(rows, 8, 1))

        left = jnp.concatenate([fields_ref[k], from_south, from_north], axis=0)
        right = jnp.concatenate([sides, ends(sides[0:8]), ends(sides[120:128])], axis=0)
        full = jnp.concatenate([left, right], axis=1)
        ext.append(jnp.where(inside, full, 0.0))
    v0, diag, along_east, along_south, cross = ext

    def laplace(u, u_l, u_r, u_u, u_d):
        return jnp.where(inside, u_l + u_r + u_u + u_d - 4.0 * u, 0.0)

    def operate(u):
        u_r = shifted(u, -1, 1)
        u_l = shifted(u, 1, 1)
        u_d = shifted(u, -1, 0)
        u_u = shifted(u, 1, 0)
        lu = laplace(u, u_l, u_r, u_u, u_d)
        near = shifted(lu, 1, 1) + shifted(lu, -1, 1) + shifted(lu, 1, 0) + shifted(lu, -1, 0)
        smooth = jnp.where(inside, (1.0 - TENSION) * near - (4.0 * (1.0 - TENSION) + TENSION) * lu, 0.0)
        u_rd = shifted(u_r, -1, 0)
        out = diag * u + along_east * u_r + along_south * u_d + cross * u_rd
        out = out + shifted(along_east * u + cross * u_d, 1, 1)
        out = out + shifted(along_south * u + cross * u_r + shifted(cross * u, 1, 1), 1, 0)
        return (out + smooth) * SHRINK

    v = [v0]
    for _ in range(3):
        v.append(operate(v[-1]))
    own = [a[0:TR, 0:TC] for a in v]
    for k in range(4):
        basis_ref[k] = own[k]
    pairs = [(0, 0), (0, 1), (1, 1), (1, 2), (2, 2), (2, 3)]
    lane = lax.broadcasted_iota(jnp.int32, (TILES, 8), 1)
    out = jnp.zeros((TILES, 8), f32)
    for k, (p, q) in enumerate(pairs):
        m = jnp.sum(jnp.sum(own[p] * own[q], axis=0, keepdims=True), axis=1, keepdims=True)
        out = jnp.where(lane == k, m, out)
    moments_ref[...] = out


def finish_kernel(moments_ref, basis_ref, surface_ref, residual_ref):
    total = jnp.sum(moments_ref[...], axis=0, keepdims=True)
    m = [total[:, k:k + 1] for k in range(6)]
    a0 = m[1] / m[0]
    sigma1 = {n: m[n + 1] - a0 * m[n] for n in range(1, 5)}
    ratio1 = sigma1[2] / sigma1[1]
    b1 = sigma1[1] / m[0]
    a1 = ratio1 - a0
    sigma2 = {n: (sigma1[n + 1] - a1 * sigma1[n]) - b1 * m[n] for n in (2, 3)}
    a2 = sigma2[3] / sigma2[2] - ratio1
    b2 = sigma2[2] / sigma1[1]
    both = a0 + a1
    flat = a0 * a1 - b1
    c2 = both + a2
    c1 = (flat + a2 * both) - b2
    third = 1.0 / (a2 * flat - b2 * a0)
    first, second = c1 * third, c2 * third
    basis = [basis_ref[k] for k in range(4)]
    surface_ref[...] = SHRINK * ((first * basis[0] - second * basis[1]) + third * basis[2])
    residual_ref[...] = ((basis[0] - first * basis[1]) + second * basis[2]) - third * basis[3]


def swaps(count):
    across = [(i, i ^ 1) for i in range(count)]
    beside = [(0, 0), (count - 1, count - 1)]
    for i in range(1, count - 1, 2):
        beside += [(i, i + 1), (i + 1, i)]
    return across, sorted(beside)


def body(destinations, cells, fractions, weights, heights, counts):
    params = pltpu.CompilerParams(vmem_limit_bytes=40 * 1024 * 1024)
    row = lax.broadcasted_iota(jnp.int32, (16, 128), 0)
    place = jnp.where(row < 8, lax.axis_index("north"), lax.axis_index("east")).astype(jnp.int32)
    block = (BLK_DEV, 128)
    send = pl.pallas_call(
        route_kernel,
        out_shape=pltpu.VMEM((TILES, 5, MOST, 128), f32),
        in_specs=[whole(pltpu.HBM), whole(pltpu.SMEM)] + [whole(pltpu.HBM)] * 4,
        out_specs=whole(),
        scratch_shapes=[
            pltpu.SMEM((BLK_DEV,), jnp.int32),
            pltpu.SMEM((TILES,), jnp.int32),
            pltpu.SMEM((BLK_DEV,), jnp.int32),
            pltpu.VMEM(block, jnp.int32),
            pltpu.VMEM((BLK_DEV, 2, 128), f32),
            pltpu.VMEM(block, f32),
            pltpu.VMEM(block, f32),
            pltpu.VMEM((5, BLK_DEV, 128), f32),
            pltpu.SemaphoreType.DMA((5,)),
        ],
        compiler_params=pltpu.CompilerParams(vmem_limit_bytes=62_050_000),
    )(destinations.reshape(BLK_DEV), counts, cells, fractions, weights, heights)
    got = lax.all_to_all(send, AXES, split_axis=0, concat_axis=0, tiled=True)
    strip = jax.ShapeDtypeStruct((5, 8, 128), f32)
    fields, top, bottom, across, beside = pl.pallas_call(
        gather_kernel,
        out_shape=[jax.ShapeDtypeStruct((5, TR, TC), f32)] + [strip] * 4,
        in_specs=[whole()] * 2,
        out_specs=[whole()] * 5,
        scratch_shapes=[
            pltpu.VMEM((PAIRS, 5, 128, 256), f32),
            pltpu.VMEM((24 * PAIRS, 128), jnp.int32),
            pltpu.SMEM((24 * PAIRS, 128), jnp.int32),
            pltpu.SMEM((3, PAIRS * STEPS * WINDOWS + 8), jnp.int32),
            pltpu.VMEM((8, 2, 28 * UNITS, 128), f32),
            pltpu.VMEM((BANDS * REACH, 128), f32),
            pltpu.SemaphoreType.DMA,
        ],
        compiler_params=params,
    )(place, got)
    east_across, east_beside = swaps(N_EAST)
    north_across, north_beside = swaps(N_NORTH)
    beside_e = lax.ppermute(beside, "east", east_beside)
    across_e = lax.ppermute(across, "east", east_across)
    message = jax.ShapeDtypeStruct((10, 8, 128), f32)
    to_across, to_beside = pl.pallas_call(
        corner_kernel,
        out_shape=[message] * 2,
        in_specs=[whole()] * 5,
        out_specs=[whole()] * 2,
        compiler_params=params,
    )(place, top, bottom, across_e, beside_e)
    beside_n = lax.ppermute(to_beside, "north", north_beside)
    across_n = lax.ppermute(to_across, "north", north_across)
    basis, moments = pl.pallas_call(
        krylov_kernel,
        out_shape=[jax.ShapeDtypeStruct((4, TR, TC), f32), jax.ShapeDtypeStruct((TILES, 8), f32)],
        in_specs=[whole()] * 6,
        out_specs=[whole()] * 2,
        compiler_params=params,
    )(place, fields, across_e, beside_e, across_n, beside_n)
    spread = lax.all_to_all(moments, AXES, split_axis=0, concat_axis=0, tiled=True)
    return pl.pallas_call(
        finish_kernel,
        out_shape=[jax.ShapeDtypeStruct((TR, TC), f32)] * 2,
        in_specs=[whole()] * 2,
        out_specs=[whole()] * 2,
        compiler_params=params,
    )(spread, basis)


def solution(mesh):
    return jax.shard_map(
        body,
        mesh=mesh,
        in_specs=(
            P(AXES, None),
            P(AXES, None),
            P(AXES, None, None),
            P(AXES, None),
            P(AXES, None),
            P(AXES),
        ),
        out_specs=(P("north", "east"), P("north", "east")),
        check_vma=False,
    )
```
